256 devices in a mesh: wide: 64 (over y, x, z_hi, core), narrow: 4 (over z_lo).
Axes of the slice: x: 4, y: 4, z: 8 (z_hi: 2, z_lo: 4; z = z_hi * 4 + z_lo), core: 2. Of those that a mesh axis runs over, the one named last changes fastest.
Arguments:
- state: float32 [262144, 1, 1024], P(('wide', 'narrow')), may hold values from -6 to 6
- col_blocks: float32 [1, 16, 128, 128], replicated, may hold values from -0.375 to 0.375
- row_blocks: float32 [1, 16, 128, 128], replicated, may hold values from -0.375 to 0.375
- col_pattern: int32 [1, 16], replicated, may hold values from 0 to 63, as said below
- row_pattern: int32 [1, 16], replicated, may hold values from 0 to 63, as said below
- qubit_order: int32 [1, 10], replicated, may hold values from 0 to 9, each once within a row
Outputs:
- amplitudes: float32 [262144, 1, 1024], P(('wide', 'narrow'))
The draws below stay inside these ranges and needn't reach their ends.
Inputs may be any that keep to these rules, and one draw needn't show every extreme that they name: `col_pattern`: each row holds 16 distinct block numbers p; among them are the 8 diagonal blocks p = 9 * b for b = 0 .. 7. `row_pattern`: each row holds 16 distinct block numbers p; among them are the 8 diagonal blocks p = 9 * b for b = 0 .. 7. `qubit_order`: each row is a permutation of 0 to 9.
All inputs are finite; a program needn't handle non-finite values.
Results may differ from the reference program's by a relative error of at most 0.0001.
Values sent between devices are 32-bit elements; how exact they have to be, the bound alone decides.
A program may use at most 128 MiB of HBM per device.

```python
import jax
import jax.numpy as jnp
from jax import lax

BLK = 128
NB = 8
ROWBITS = 10
NNZ = 16
LAYERS = 1
SLABS = 1
ORDER = 1024
N_WIDE = 64
N_NARROW = 4


def block_pattern(key):

    def one_gate(subkey):
        first_key, second_key = jax.random.split(subkey)
        ranks = jax.random.permutation(first_key, NB * NB - NB)[:NNZ - NB].astype(jnp.int32)
        block_row = ranks // (NB - 1)
        other = ranks % (NB - 1)
        block_col = other + (other >= block_row).astype(jnp.int32)
        offdiag = block_row * NB + block_col
        diagonal = jnp.arange(NB, dtype=jnp.int32) * (NB + 1)
        joined = jnp.concatenate([diagonal, offdiag]).astype(jnp.int32)
        return jax.random.permutation(second_key, joined).astype(jnp.int32)
    return jax.vmap(one_gate)(jax.random.split(key, LAYERS))


def draw_col_pattern(key, part):
    return block_pattern(jax.random.fold_in(key, 101))


def draw_row_pattern(key, part):
    return block_pattern(jax.random.fold_in(key, 202))


def level_of(key, shape, cuts, least, high):
    loudness, own = 1.0, jax.random.fold_in(key, 6)
    for position, blocks in cuts:
        steps = jnp.exp(jax.random.uniform(jax.random.fold_in(own, position), (blocks,), jnp.float32, least / len(cuts), high / len(cuts)))
        loudness = loudness * jnp.repeat(steps, shape[position] // blocks).reshape([-1 if axis == position else 1 for axis in range(len(shape))])
    return loudness


def scatter_about(own_key, extent, deviation, most, pieces=(), kind=jnp.bfloat16):
    array = deviation * jax.random.normal(own_key, extent, jnp.float32)
    if pieces:
        array = array * level_of(own_key, extent, pieces, -0.22, 0.18)
    return jnp.clip(array, -most, most).astype(kind)


def setup_inputs(seed: int = 0) -> dict:
    streams_of = jax.random.split(jax.random.key(seed), 7)
    state = scatter_about(streams_of[0], (N_WIDE * N_NARROW * ORDER, SLABS, ORDER), 1.0, 6.0, ((0, 256),), jnp.float32)
    col_blocks = scatter_about(streams_of[1], (LAYERS, NNZ, BLK, BLK), (2 * BLK) ** -0.5, 0.375, (), jnp.float32)
    row_blocks = scatter_about(streams_of[2], (LAYERS, NNZ, BLK, BLK), (2 * BLK) ** -0.5, 0.375, (), jnp.float32)
    col_pattern = draw_col_pattern(jax.random.fold_in(streams_of[6], 71), 0)
    row_pattern = draw_row_pattern(jax.random.fold_in(streams_of[6], 71), 0)
    qubit_order = jax.vmap(lambda own: jax.random.permutation(own, ROWBITS))(jax.random.split(streams_of[5], LAYERS)).reshape((LAYERS, ROWBITS)).astype(jnp.int32)
    return {"state": state, "col_blocks": col_blocks, "row_blocks": row_blocks, "col_pattern": col_pattern, "row_pattern": row_pattern, "qubit_order": qubit_order}


HIGHEST = lax.Precision.HIGHEST


def column_gate(amplitudes, blocks, pattern):
    block_size = blocks.shape[1]
    groups = amplitudes.shape[-1] // block_size
    leading = amplitudes.shape[:-1]
    grouped = amplitudes.reshape(leading + (groups, block_size))
    picked = jnp.take(grouped, (pattern % groups).astype(jnp.int32), axis=-2)
    blended = jnp.einsum("...ke,kde->...kd", picked, blocks, precision=HIGHEST)
    placer = ((pattern[:, None] // groups) == jnp.arange(groups, dtype=jnp.int32)[None, :]).astype(jnp.float32)
    placed = jnp.einsum("...kd,kb->...bd", blended, placer, precision=HIGHEST)
    return placed.reshape(amplitudes.shape)


def row_gate(amplitudes, blocks, pattern):
    block_size = blocks.shape[1]
    groups = amplitudes.shape[0] // block_size
    grouped = amplitudes.reshape(groups, block_size, -1)
    picked = jnp.take(grouped, (pattern % groups).astype(jnp.int32), axis=0)
    blended = jnp.einsum("kde,kem->kdm", blocks, picked, precision=HIGHEST)
    placer = ((pattern[:, None] // groups) == jnp.arange(groups, dtype=jnp.int32)[None, :]).astype(jnp.float32)
    placed = jnp.einsum("kb,kdm->bdm", placer, blended, precision=HIGHEST)
    return placed.reshape(amplitudes.shape)


def relabel_source(ordering, row_total):
    positions = jnp.arange(row_total, dtype=jnp.int32)
    qubits = jnp.arange(ordering.shape[0], dtype=jnp.int32)
    digits = (positions[:, None] >> qubits[None, :]) & 1
    return jnp.sum(digits << ordering[None, :].astype(jnp.int32), axis=1).astype(jnp.int32)


def reference(state, col_blocks, row_blocks, col_pattern, row_pattern, qubit_order):
    wide_bits = N_WIDE.bit_length() - 1
    devices_all = N_WIDE * N_NARROW
    current = state.reshape(devices_all, ORDER, SLABS, ORDER)
    for layer_index in range(LAYERS):
        rblocks = row_blocks[layer_index]
        rpattern = row_pattern[layer_index]
        current = lax.map(lambda shard: row_gate(shard, rblocks, rpattern), current)
        source = relabel_source(qubit_order[layer_index], ORDER)
        current = jnp.take(current, source, axis=1)
        qubit = wide_bits - 1 - layer_index
        shaped = current.reshape(N_WIDE >> (qubit + 1), 2, (1 << qubit) * N_NARROW, 2, ORDER // 2, SLABS, ORDER)
        current = jnp.swapaxes(shaped, 1, 3).reshape(devices_all, ORDER, SLABS, ORDER)
        if layer_index + 1 < LAYERS:
            cblocks = col_blocks[layer_index]
            cpattern = col_pattern[layer_index]
            current = lax.map(lambda shard: column_gate(shard, cblocks, cpattern), current)
    shaped = current.reshape(N_WIDE, N_NARROW, N_NARROW, ORDER // N_NARROW, SLABS, ORDER)
    current = jnp.swapaxes(shaped, 1, 2).reshape(devices_all, ORDER, SLABS, ORDER)
    fblocks = col_blocks[LAYERS - 1]
    fpattern = col_pattern[LAYERS - 1]
    current = lax.map(lambda shard: column_gate(shard, fblocks, fpattern), current)
    return current.reshape(devices_all * ORDER, SLABS, ORDER)
```

```python
import functools

import jax
import jax.numpy as jnp
from jax import lax
from jax.experimental import pallas as pl
from jax.experimental.pallas import tpu as pltpu
from jax.sharding import PartitionSpec as P

MESH = pl.DeviceIdType.MESH
F32, BF16 = jnp.float32, jnp.bfloat16
N = 1024
LANES = 128
TILES = 8
HALF = 64
PIECES = 4
PIECE = HALF // PIECES


def split(value):
    hi = value.astype(BF16)
    lo = (value - hi.astype(F32)).astype(BF16)
    return hi, lo


def prepare(
    x_hbm, cb_hbm, rb_hbm, cpat_hbm, rpat_hbm, order_hbm,
    xhi, xlo, ghi, glo, hhi, hlo, weights,
    xv, cbv, rbv, cpat, rpat, order, sem,
):
    parts = 4
    rows = N // parts
    rcopy = pltpu.make_async_copy(rb_hbm, rbv, sem.at[0])
    ccopy = pltpu.make_async_copy(cb_hbm, cbv, sem.at[1])
    small = [
        pltpu.make_async_copy(source, target, sem.at[6 + q])
        for q, (source, target) in enumerate(((rpat_hbm, rpat), (cpat_hbm, cpat), (order_hbm, order)))
    ]
    for copy in small:
        copy.start()
    rcopy.start()
    copies = []
    for part in range(parts):
        where = pl.ds(part * rows * 8, rows * 8)
        copies.append(pltpu.make_async_copy(x_hbm.at[where], xv.at[where], sem.at[2 + part]))
        copies[-1].start()
    ccopy.start()
    zero = jnp.zeros((128, N), BF16)

    @pl.loop(0, 8)
    def _(i):
        where = pl.ds(pl.multiple_of(i * 128, 128), 128)
        for ref in (ghi, glo, hhi, hlo):
            ref[where, :] = zero

    def place(blocks, pattern, hi_ref, lo_ref):
        @pl.loop(0, 16)
        def _(k):
            p = pattern[0, k]
            row = pl.ds(pl.multiple_of((p // 8) * 128, 128), 128)
            col = pl.ds(pl.multiple_of((p % 8) * 128, 128), 128)
            hi, lo = split(blocks[pl.ds(pl.multiple_of(k * 128, 128), 128), :])
            hi_ref[row, col] = hi
            lo_ref[row, col] = lo

    for copy in small:
        copy.wait()
    lane = lax.broadcasted_iota(jnp.int32, (8, LANES), 1)
    value = jnp.zeros((8, LANES), jnp.int32)
    for q in range(10):
        value = jnp.where(lane == q, 1 << order[0, q], value)
    weights[...] = value
    rcopy.wait()
    place(rbv, rpat, ghi, glo)
    for part in range(parts):
        copies[part].wait()

        @pl.loop(0, rows // 64)
        def _(i):
            r0 = pl.multiple_of(part * rows + i * 64, 64)
            for ct in range(8):
                hi, lo = split(xv[pl.ds(r0 * 8 + ct, 64, stride=8), :])
                xhi[pl.ds(r0, 64), ct * 128:(ct + 1) * 128] = hi
                xlo[pl.ds(r0, 64), ct * 128:(ct + 1) * 128] = lo

    ccopy.wait()
    place(cbv, cpat, hhi, hlo)


def exchange(xhi, xlo, ghi, glo, hhi, hlo, weights, out, ytile, ybuf, ssem, ysem, zsem, lsem, *, half_wide):
    w, n = lax.axis_index("wide"), lax.axis_index("narrow")
    w5, wl = w // half_wide, w % half_wide
    n1, n0 = n // 2, n % 2
    near = (w5, n)

    def place_of(a, b):
        return (a * half_wide + wl, b)

    barrier = pltpu.get_barrier_semaphore()
    pl.semaphore_signal(barrier, inc=1, device_id=place_of(1 - w5, n), device_id_type=MESH)
    for j in range(1, 4):
        pl.semaphore_signal(barrier, inc=1, device_id=place_of(w5, lax.rem(n + j, 4)), device_id_type=MESH)

    def rows8(start, count):
        return pl.ds(pl.multiple_of(start * 8, 8), count * 8)

    def compute(i):
        r8, j = i % 2, i // 2
        m = lax.broadcasted_iota(jnp.int32, (2 * HALF, 1), 0)
        away = m // HALF
        top = w5 + away - 2 * w5 * away
        r = top * 512 + r8 * 256 + j * HALF + m % HALF
        lane = lax.broadcasted_iota(jnp.int32, (2 * HALF, LANES), 1)
        bits = lax.shift_right_logical(jnp.broadcast_to(r, (2 * HALF, LANES)), jnp.minimum(lane, 31)) & 1
        source = jnp.sum((bits * weights[0:1, :]).astype(F32), axis=1, keepdims=True).astype(jnp.int32)
        onehot = (lax.broadcasted_iota(jnp.int32, (2 * HALF, N), 1) == source).astype(F32).astype(BF16)
        g_hi = jnp.dot(onehot, ghi[...], preferred_element_type=F32).astype(BF16)
        g_lo = jnp.dot(onehot, glo[...], preferred_element_type=F32).astype(BF16)
        g2 = jnp.concatenate([g_hi, g_lo], axis=0)
        big = jnp.dot(g2, xhi[...], preferred_element_type=F32)
        z = big[:128] + big[128:] + jnp.dot(g_hi, xlo[...], preferred_element_type=F32)
        z_hi, z_lo = split(z)
        z2 = jnp.concatenate([z_hi, z_lo], axis=0)
        nt = (((1,), (1,)), ((), ()))
        big = lax.dot_general(z2, hhi[...], nt, preferred_element_type=F32)
        y = big[:128] + big[128:] + lax.dot_general(z_hi, hlo[...], nt, preferred_element_type=F32)
        base = pl.multiple_of(i * 1024, 1024)
        for ct in range(8):
            ytile[pl.ds(base + ct, 2 * HALF, stride=8), :] = y[:, ct * 128:(ct + 1) * 128]

    def spot(i):
        return (i % 2) * 256 + (i // 2) * HALF

    def send(i):
        r8, j = i % 2, i // 2
        direct = (n1 == w5) & (n0 == r8)
        for p in range(PIECES):
            src = ytile.at[rows8(i * 128 + HALF + p * PIECE, PIECE)]

            def to(dst, src=src, p=p):
                pltpu.make_async_remote_copy(
                    src_ref=src, dst_ref=dst, send_sem=ssem.at[0], recv_sem=ysem.at[i * PIECES + p],
                    device_id=place_of(1 - w5, n), device_id_type=MESH,
                ).start()

            @pl.when(direct)
            def _():
                to(out.at[rows8(n * 256 + j * HALF + p * PIECE, PIECE)])

            @pl.when(jnp.logical_not(direct))
            def _():
                to(ybuf.at[rows8(spot(i) + p * PIECE, PIECE)])

        mine = ytile.at[rows8(i * 128, HALF)]
        where = out.at[rows8(n * 256 + j * HALF, HALF)]

        @pl.when(direct)
        def _():
            pltpu.make_async_copy(mine, where, lsem.at[0]).start()

        @pl.when(jnp.logical_not(direct))
        def _():
            pltpu.make_async_remote_copy(
                src_ref=mine, dst_ref=where, send_sem=ssem.at[1], recv_sem=zsem.at[0],
                device_id=place_of(w5, 2 * w5 + r8), device_id_type=MESH,
            ).start()

    def forward(i, p):
        r8, j = i % 2, i // 2
        src = ybuf.at[rows8(spot(i) + p * PIECE, PIECE)]
        pltpu.make_async_copy(src, src, ysem.at[i * PIECES + p]).wait()

        @pl.when(jnp.logical_not((n1 != w5) & (n0 == r8)))
        def _():
            pltpu.make_async_remote_copy(
                src_ref=src, dst_ref=out.at[rows8(n * 256 + j * HALF + p * PIECE, PIECE)],
                send_sem=ssem.at[2], recv_sem=zsem.at[0],
                device_id=place_of(w5, 2 * (1 - w5) + r8), device_id_type=MESH,
            ).start()

    compute(0)
    pl.semaphore_wait(barrier, 4)
    send(0)
    forward(0, 0)

    @pl.loop(1, TILES)
    def _(i):
        compute(i)
        send(i)

        @pl.when(i > 1)
        def _():
            forward(i - 1, 0)

        for p in range(1, PIECES):
            forward(i - 1, p)

    for p in range(PIECES):
        forward(TILES - 1, p)

    def drain(rows, sem):
        ref = ytile.at[pl.ds(0, rows * 8)]
        pltpu.make_async_copy(ref, ref, sem).wait()

    drain(512, ssem.at[0])

    @pl.when(n1 == w5)
    def _():
        drain(256, lsem.at[0])
        drain(256, ssem.at[1])
        drain(512, ssem.at[2])

    @pl.when(n1 != w5)
    def _():
        drain(512, ssem.at[1])
        drain(256, ssem.at[2])

    drain(768, zsem.at[0])


def solution(mesh):
    half_wide = mesh.shape["wide"] // 2
    vmem = pl.BlockSpec(memory_space=pltpu.VMEM)
    hbm = pl.BlockSpec(memory_space=pltpu.HBM)

    def local(state, col_blocks, row_blocks, col_pattern, row_pattern, qubit_order):
        square = jax.ShapeDtypeStruct((N, N), BF16)
        parts = pl.pallas_call(
            prepare,
            out_shape=(square,) * 6 + (jax.ShapeDtypeStruct((8, LANES), jnp.int32),),
            in_specs=[hbm] * 6,
            out_specs=(vmem,) * 7,
            scratch_shapes=[
                pltpu.VMEM((8 * N, LANES), F32),
                pltpu.VMEM((2048, LANES), F32),
                pltpu.VMEM((2048, LANES), F32),
                pltpu.SMEM((1, 16), jnp.int32),
                pltpu.SMEM((1, 16), jnp.int32),
                pltpu.SMEM((1, 10), jnp.int32),
                pltpu.SemaphoreType.DMA((9,)),
            ],
            compiler_params=pltpu.CompilerParams(vmem_limit_bytes=24 << 20),
        )(
            *(
                pltpu.with_memory_space_constraint(value, pltpu.HBM)
                for value in (
                    state.reshape(8 * N, LANES),
                    col_blocks.reshape(2048, LANES),
                    row_blocks.reshape(2048, LANES),
                    col_pattern,
                    row_pattern,
                    qubit_order,
                )
            )
        )
        result = pl.pallas_call(
            functools.partial(exchange, half_wide=half_wide),
            out_shape=jax.ShapeDtypeStruct((8 * N, LANES), F32),
            in_specs=[vmem] * 7,
            out_specs=vmem,
            scratch_shapes=[
                pltpu.VMEM((8 * N, LANES), F32),
                pltpu.VMEM((4 * N, LANES), F32),
                pltpu.SemaphoreType.DMA((3,)),
                pltpu.SemaphoreType.DMA((TILES * PIECES,)),
                pltpu.SemaphoreType.DMA((1,)),
                pltpu.SemaphoreType.DMA((1,)),
            ],
            compiler_params=pltpu.CompilerParams(
                collective_id=0, has_side_effects=True, vmem_limit_bytes=32 << 20
            ),
        )(*parts)
        return result.reshape(N, 1, N)

    return jax.shard_map(
        local,
        mesh=mesh,
        in_specs=(P(("wide", "narrow"), None, None), P(), P(), P(), P(), P()),
        out_specs=P(("wide", "narrow"), None, None),
        check_vma=False,
    )
```

```python
import functools

import jax
import jax.numpy as jnp
from jax import lax
from jax.experimental import pallas as pl
from jax.experimental.pallas import tpu as pltpu
from jax.sharding import PartitionSpec as P

MESH = pl.DeviceIdType.MESH
F32, BF16 = jnp.float32, jnp.bfloat16
N = 1024
LANES = 128
NNZ = 16
TILES = 8
HALF = 64
PIECES = 4
PIECE = HALF // PIECES
SLAB = N // PIECES


def split(value):
    hi = value.astype(BF16)
    lo = (value - hi.astype(F32)).astype(BF16)
    return hi, lo


def exchange(
    x_hbm, cb_hbm, rb_hbm, cpat_hbm, rpat_hbm, order_hbm, out,
    cpat, rpat, order, rbv, cbv, xraw, xhi, xlo, bcat, ccat, hhi, hlo, diff, acat,
    zs, zy, zin, ytile, ybuf, insem, ssem, ysem, zsem, zinsem, lsem, *, half_wide,
):
    w, n = lax.axis_index("wide"), lax.axis_index("narrow")
    w5, wl = w // half_wide, w % half_wide
    n1, n0 = n // 2, n % 2

    def place_of(a, b):
        return (a * half_wide + wl, b)

    barrier = pltpu.get_barrier_semaphore()
    pl.semaphore_signal(barrier, inc=1, device_id=place_of(1 - w5, n), device_id_type=MESH)
    for j in range(1, 4):
        pl.semaphore_signal(barrier, inc=1, device_id=place_of(w5, lax.rem(n + j, 4)), device_id_type=MESH)

    def block(k):
        return pl.ds(pl.multiple_of(k * 128, 128), 128)

    def rows8(start, count):
        return pl.ds(pl.multiple_of(start * 8, 8), count * 8)

    def slab_copy(s):
        columns = pl.ds(pl.multiple_of(s * SLAB, SLAB), SLAB)
        return pltpu.make_async_copy(x_hbm.at[:, 0, columns], xraw.at[s], insem.at[s])

    small = [
        pltpu.make_async_copy(source, target, insem.at[PIECES + q])
        for q, (source, target) in enumerate(((rpat_hbm, rpat), (cpat_hbm, cpat), (order_hbm, order)))
    ]
    rcopy = pltpu.make_async_copy(rb_hbm, rbv, insem.at[PIECES + 3])
    ccopy = pltpu.make_async_copy(cb_hbm, cbv, insem.at[PIECES + 4])
    for copy in small:
        copy.start()
    rcopy.start()
    for s in range(PIECES):
        slab_copy(s).start()
    ccopy.start()
    for copy in small:
        copy.wait()

    m = lax.broadcasted_iota(jnp.int32, (2 * HALF, LANES), 0)
    away = m // HALF
    label = (w5 + away - 2 * w5 * away) * (1 << order[0, 9])
    for q in range(6):
        label = label + ((m // (2**q)) % 2) * (1 << order[0, q])
    diff[...] = label - lax.broadcasted_iota(jnp.int32, (2 * HALF, LANES), 1)

    def pack(source, target):
        @pl.loop(0, NNZ)
        def _(k):
            hi, lo = split(source[block(k), :])
            target[block(k), 0:LANES] = hi
            target[block(k), LANES:2 * LANES] = lo

    def mixing(i):
        r8, j = i % 2, i // 2
        base = r8 * (1 << order[0, 8]) + (j % 2) * (1 << order[0, 6]) + (j // 2) * (1 << order[0, 7])
        for k in range(NNZ):
            onehot = (diff[...] == (rpat[0, k] >> 3) * 128 - base).astype(F32).astype(BF16)
            mixed = jnp.dot(onehot, bcat[k * 128:(k + 1) * 128, :], preferred_element_type=F32).astype(BF16)
            acat[0:128, k * 128:(k + 1) * 128] = mixed[:, :LANES]
            acat[128:256, k * 128:(k + 1) * 128] = mixed[:, LANES:]

    def row_gate(columns):
        total = None
        for k in range(0, NNZ, 2):
            left = acat[:, k * 128:(k + 2) * 128]
            first, second = pl.ds((rpat[0, k] & 7) * 128, 128), pl.ds((rpat[0, k + 1] & 7) * 128, 128)
            right = jnp.concatenate([xhi[first, columns], xhi[second, columns]], axis=0)
            both = jnp.dot(left, right, preferred_element_type=F32)
            right = jnp.concatenate([xlo[first, columns], xlo[second, columns]], axis=0)
            term = both[:128] + both[128:] + jnp.dot(left[:128], right, preferred_element_type=F32)
            total = term if total is None else total + term
        return total

    def column_gate(z):
        z_hi, z_lo = split(z)
        both = jnp.concatenate([z_hi, z_lo], axis=0)
        turned = (((1,), (1,)), ((), ()))
        both = lax.dot_general(both, hhi[...], turned, preferred_element_type=F32)
        return both[:128] + both[128:] + lax.dot_general(z_hi, hlo[...], turned, preferred_element_type=F32)

    def to_y(source, target, index):
        pltpu.make_async_remote_copy(
            src_ref=source, dst_ref=target, send_sem=ssem.at[0], recv_sem=ysem.at[index],
            device_id=place_of(1 - w5, n), device_id_type=MESH,
        ).start()

    def to_z(source, target, which, sem, column):
        pltpu.make_async_remote_copy(
            src_ref=source, dst_ref=target, send_sem=ssem.at[which], recv_sem=sem,
            device_id=place_of(w5, column), device_id_type=MESH,
        ).start()

    def make_slab(s):
        columns = pl.ds(pl.multiple_of(s * SLAB, SLAB), SLAB)
        slab_copy(s).wait()

        @pl.loop(0, N // 128)
        def _(b):
            hi, lo = split(xraw[s, block(b), :])
            xhi[block(b), columns] = hi
            xlo[block(b), columns] = lo

        zs[s] = row_gate(columns)

    def send_slab(s):
        direct = (n1 == w5) & (n0 == 0)
        away_part, own_part = zs.at[s, pl.ds(HALF, HALF)], zs.at[s, pl.ds(0, HALF)]

        @pl.when(direct)
        def _():
            to_y(away_part, zin.at[n, s], s)
            pltpu.make_async_copy(own_part, zin.at[n, s], lsem.at[0]).start()

        @pl.when(jnp.logical_not(direct))
        def _():
            to_y(away_part, zy.at[s], s)
            to_z(own_part, zin.at[n, s], 1, zinsem.at[n], 2 * w5)

    def forward_slab(s):
        pltpu.make_async_copy(zy.at[s], zy.at[s], ysem.at[s]).wait()

        @pl.when(jnp.logical_not((n1 != w5) & (n0 == 0)))
        def _():
            to_z(zy.at[s], zin.at[n, s], 2, zinsem.at[n], 2 * (1 - w5))

    def make_tile(i):
        mixing(i)
        y = column_gate(row_gate(slice(0, N)))
        base = pl.multiple_of(i * 1024, 1024)
        for ct in range(8):
            ytile[pl.ds(base + ct, 2 * HALF, stride=8), :] = y[:, ct * 128:(ct + 1) * 128]

    def spot(i):
        return (i % 2) * 256 + (i // 2) * HALF

    def send_tile(i):
        r8, j = i % 2, i // 2
        direct = (n1 == w5) & (n0 == r8)
        mine = ytile.at[rows8(i * 128, HALF)]
        where = out.at[rows8(n * 256 + j * HALF, HALF)]
        for p in range(PIECES):
            source = ytile.at[rows8(i * 128 + HALF + p * PIECE, PIECE)]

            @pl.when(direct)
            def _():
                to_y(source, out.at[rows8(n * 256 + j * HALF + p * PIECE, PIECE)], i * PIECES + p)

            @pl.when(jnp.logical_not(direct))
            def _():
                to_y(source, ybuf.at[rows8(spot(i) + p * PIECE, PIECE)], i * PIECES + p)

        @pl.when(direct)
        def _():
            pltpu.make_async_copy(mine, where, lsem.at[0]).start()

        @pl.when(jnp.logical_not(direct))
        def _():
            to_z(mine, where, 1, zsem.at[0], 2 * w5 + r8)

    def forward(i, p):
        r8, j = i % 2, i // 2
        source = ybuf.at[rows8(spot(i) + p * PIECE, PIECE)]
        pltpu.make_async_copy(source, source, ysem.at[i * PIECES + p]).wait()

        @pl.when(jnp.logical_not((n1 != w5) & (n0 == r8)))
        def _():
            target = out.at[rows8(n * 256 + j * HALF + p * PIECE, PIECE)]
            to_z(source, target, 2, zsem.at[0], 2 * (1 - w5) + r8)

    rcopy.wait()
    pack(rbv, bcat)
    mixing(0)
    make_slab(0)
    pl.semaphore_wait(barrier, 4)
    send_slab(0)

    @pl.loop(1, PIECES)
    def _(s):
        make_slab(s)
        send_slab(s)

    forward_slab(0)
    ccopy.wait()
    pack(cbv, ccat)
    ccat[NNZ * 128:(NNZ + 1) * 128, :] = jnp.zeros((128, 2 * LANES), BF16)

    @pl.loop(0, 64)
    def _(q):
        found = NNZ
        for k in range(NNZ):
            found = found + (cpat[0, k] == q).astype(jnp.int32) * (k - NNZ)
        value = ccat[pl.ds((found & (2 * NNZ - 1)) * 128, 128), :]
        hhi[block(q // 8), block(q % 8)] = value[:, :LANES]
        hlo[block(q // 8), block(q % 8)] = value[:, LANES:]

    forward_slab(1)
    forward_slab(2)

    @pl.loop(1, TILES)
    def _(i):
        make_tile(i)
        send_tile(i)

        @pl.when(i == 1)
        def _():
            forward_slab(3)

        @pl.when(i > 1)
        def _():
            for p in range(PIECES):
                forward(i - 1, p)

    for p in range(PIECES):
        forward(TILES - 1, p)

    def drain(rows, sem):
        ref = ytile.at[pl.ds(0, rows * 8)]
        pltpu.make_async_copy(ref, ref, sem).wait()

    @pl.when(n1 == w5)
    def _():
        drain(256, lsem.at[0])

    @pl.when(n0 == 0)
    def _():
        for q in range(4):
            @pl.when(n != q)
            def _():
                pltpu.make_async_copy(zin.at[q], zin.at[q], zinsem.at[q]).wait()

        @pl.loop(0, 2)
        def _(pair):
            z = jnp.concatenate(
                [
                    jnp.concatenate([zin[2 * pair + h, s] for s in range(PIECES)], axis=1)
                    for h in range(2)
                ],
                axis=0,
            )
            y = column_gate(z)
            for h in range(2):
                base = pl.multiple_of((2 * pair + h) * 2048, 2048)
                for ct in range(8):
                    out[pl.ds(base + ct, HALF, stride=8), :] = y[h * HALF:(h + 1) * HALF, ct * 128:(ct + 1) * 128]

    drain(512, ssem.at[0])

    @pl.when(n1 == w5)
    def _():
        drain(256, ssem.at[1])
        drain(512, ssem.at[2])

    @pl.when(n1 != w5)
    def _():
        drain(512, ssem.at[1])
        drain(256, ssem.at[2])

    @pl.when(n0 == 0)
    def _():
        drain(576, zsem.at[0])

    @pl.when(n0 == 1)
    def _():
        drain(768, zsem.at[0])


def solution(mesh):
    half_wide = mesh.shape["wide"] // 2
    hbm = pl.BlockSpec(memory_space=pltpu.HBM)

    def local(state, col_blocks, row_blocks, col_pattern, row_pattern, qubit_order):
        result = pl.pallas_call(
            functools.partial(exchange, half_wide=half_wide),
            out_shape=jax.ShapeDtypeStruct((8 * N, LANES), F32),
            in_specs=[hbm] * 6,
            out_specs=pl.BlockSpec(memory_space=pltpu.VMEM),
            scratch_shapes=[
                pltpu.SMEM((1, NNZ), jnp.int32),
                pltpu.SMEM((1, NNZ), jnp.int32),
                pltpu.SMEM((1, 10), jnp.int32),
                pltpu.VMEM((NNZ * 128, LANES), F32),
                pltpu.VMEM((NNZ * 128, LANES), F32),
                pltpu.VMEM((PIECES, N, SLAB), F32),
                pltpu.VMEM((N, N), BF16),
                pltpu.VMEM((N, N), BF16),
                pltpu.VMEM((NNZ * 128, 2 * LANES), BF16),
                pltpu.VMEM((2 * NNZ * 128, 2 * LANES), BF16),
                pltpu.VMEM((N, N), BF16),
                pltpu.VMEM((N, N), BF16),
                pltpu.VMEM((2 * HALF, LANES), jnp.int32),
                pltpu.VMEM((256, NNZ * 128), BF16),
                pltpu.VMEM((PIECES, 2 * HALF, SLAB), F32),
                pltpu.VMEM((PIECES, HALF, SLAB), F32),
                pltpu.VMEM((4, PIECES, HALF, SLAB), F32),
                pltpu.VMEM((8 * N, LANES), F32),
                pltpu.VMEM((4 * N, LANES), F32),
                pltpu.SemaphoreType.DMA((PIECES + 5,)),
                pltpu.SemaphoreType.DMA((3,)),
                pltpu.SemaphoreType.DMA((TILES * PIECES,)),
                pltpu.SemaphoreType.DMA((1,)),
                pltpu.SemaphoreType.DMA((4,)),
                pltpu.SemaphoreType.DMA((1,)),
            ],
            compiler_params=pltpu.CompilerParams(
                collective_id=0, has_side_effects=True, vmem_limit_bytes=48 << 20
            ),
        )(
            *(
                pltpu.with_memory_space_constraint(value, pltpu.HBM)
                for value in (
                    state,
                    col_blocks.reshape(NNZ * 128, LANES),
                    row_blocks.reshape(NNZ * 128, LANES),
                    col_pattern,
                    row_pattern,
                    qubit_order,
                )
            )
        )
        return result.reshape(N, 1, N)

    return jax.shard_map(
        local,
        mesh=mesh,
        in_specs=(P(("wide", "narrow"), None, None), P(), P(), P(), P(), P()),
        out_specs=P(("wide", "narrow"), None, None),
        check_vma=False,
    )
```

```python
import functools

import jax
import jax.numpy as jnp
from jax import lax
from jax.experimental import pallas as pl
from jax.experimental.pallas import tpu as pltpu
from jax.sharding import PartitionSpec as P

MESH = pl.DeviceIdType.MESH
F32, BF16 = jnp.float32, jnp.bfloat16
N = 1024
LANES = 128
NNZ = 16
TILES = 8
HALF = 64
PIECES = 4
PIECE = HALF // PIECES
SLAB = N // PIECES
FIRST = PIECES + 1
STRAIGHT = 6


def split(value):
    hi = value.astype(BF16)
    lo = (value - hi.astype(F32)).astype(BF16)
    return hi, lo


def exchange(
    x_hbm, cb_hbm, rb_hbm, cpat_hbm, rpat_hbm, order_hbm, out,
    cpat, rpat, order, rbv, cbv, xraw, xhi, xlo, bcat, ccat, hhi, hlo, diff, acat,
    zs, zy, zin, ytile, ybuf, insem, ssem, ysem, zsem, zinsem, lsem, *, half_wide,
):
    w, n = lax.axis_index("wide"), lax.axis_index("narrow")
    w5, wl = w // half_wide, w % half_wide
    n1, n0 = n // 2, n % 2

    def place_of(a, b):
        return (a * half_wide + wl, b)

    barrier = pltpu.get_barrier_semaphore()
    pl.semaphore_signal(barrier, inc=1, device_id=place_of(1 - w5, n), device_id_type=MESH)
    for j in range(1, 4):
        pl.semaphore_signal(barrier, inc=1, device_id=place_of(w5, lax.rem(n + j, 4)), device_id_type=MESH)

    @pl.when(n1 != w5)
    def _():
        for j in range(2):
            pl.semaphore_signal(barrier, inc=1, device_id=place_of(1 - w5, 2 * w5 + j), device_id_type=MESH)

    def block(k):
        return pl.ds(pl.multiple_of(k * 128, 128), 128)

    def rows8(start, count):
        return pl.ds(pl.multiple_of(start * 8, 8), count * 8)

    def slab_copy(s):
        columns = pl.ds(pl.multiple_of(s * SLAB, SLAB), SLAB)
        return pltpu.make_async_copy(x_hbm.at[:, 0, columns], xraw.at[s], insem.at[s])

    def half_copy(h):
        return pltpu.make_async_copy(
            x_hbm.at[:, 0, pl.ds(h * 128, 128)], xraw.at[0, :, pl.ds(h * 128, 128)], insem.at[PIECES * h]
        )

    small = [
        pltpu.make_async_copy(source, target, insem.at[FIRST + q])
        for q, (source, target) in enumerate(((rpat_hbm, rpat), (cpat_hbm, cpat), (order_hbm, order)))
    ]
    rcopy = pltpu.make_async_copy(rb_hbm, rbv, insem.at[FIRST + 3])
    ccopy = pltpu.make_async_copy(cb_hbm, cbv, insem.at[FIRST + 4])
    for copy in small:
        copy.start()
    rcopy.start()
    for h in range(2):
        half_copy(h).start()
    for s in range(1, PIECES):
        slab_copy(s).start()
    ccopy.start()
    for copy in small:
        copy.wait()

    m = lax.broadcasted_iota(jnp.int32, (2 * HALF, LANES), 0)
    away = m // HALF
    label = (w5 + away - 2 * w5 * away) * (1 << order[0, 9])
    for q in range(6):
        label = label + ((m // (2**q)) % 2) * (1 << order[0, q])
    diff[...] = label - lax.broadcasted_iota(jnp.int32, (2 * HALF, LANES), 1)

    def pack(source, target):
        @pl.loop(0, NNZ)
        def _(k):
            hi, lo = split(source[block(k), :])
            target[block(k), 0:LANES] = hi
            target[block(k), LANES:2 * LANES] = lo

    def mixing(i):
        r8, j = i % 2, i // 2
        base = r8 * (1 << order[0, 8]) + (j % 2) * (1 << order[0, 6]) + (j // 2) * (1 << order[0, 7])
        for k in range(NNZ):
            onehot = (diff[...] == (rpat[0, k] >> 3) * 128 - base).astype(F32).astype(BF16)
            mixed = jnp.dot(onehot, bcat[k * 128:(k + 1) * 128, :], preferred_element_type=F32).astype(BF16)
            acat[0:128, k * 128:(k + 1) * 128] = mixed[:, :LANES]
            acat[128:256, k * 128:(k + 1) * 128] = mixed[:, LANES:]

    def row_gate(columns):
        total = None
        for k in range(0, NNZ, 2):
            left = acat[:, k * 128:(k + 2) * 128]
            first, second = pl.ds((rpat[0, k] & 7) * 128, 128), pl.ds((rpat[0, k + 1] & 7) * 128, 128)
            right = jnp.concatenate([xhi[first, columns], xhi[second, columns]], axis=0)
            both = jnp.dot(left, right, preferred_element_type=F32)
            right = jnp.concatenate([xlo[first, columns], xlo[second, columns]], axis=0)
            term = both[:128] + both[128:] + jnp.dot(left[:128], right, preferred_element_type=F32)
            total = term if total is None else total + term
        return total

    def column_gate(z):
        z_hi, z_lo = split(z)
        both = jnp.concatenate([z_hi, z_lo], axis=0)
        turned = (((1,), (1,)), ((), ()))
        both = lax.dot_general(both, hhi[...], turned, preferred_element_type=F32)
        return both[:128] + both[128:] + lax.dot_general(z_hi, hlo[...], turned, preferred_element_type=F32)

    def to_y(source, target, index):
        pltpu.make_async_remote_copy(
            src_ref=source, dst_ref=target, send_sem=ssem.at[0], recv_sem=ysem.at[index],
            device_id=place_of(1 - w5, n), device_id_type=MESH,
        ).start()

    def to_z(source, target, which, sem, column):
        pltpu.make_async_remote_copy(
            src_ref=source, dst_ref=target, send_sem=ssem.at[which], recv_sem=sem,
            device_id=place_of(w5, column), device_id_type=MESH,
        ).start()

    def make_part(s, lanes, copy):
        columns = pl.ds(pl.multiple_of(s * SLAB + lanes.start, 128), lanes.size)
        copy.wait()

        @pl.loop(0, N // 128)
        def _(b):
            hi, lo = split(xraw[s, block(b), lanes])
            xhi[block(b), columns] = hi
            xlo[block(b), columns] = lo

        zs[s, :, lanes] = row_gate(columns)

    def send_part(s, lanes, index):
        direct = (n1 == w5) & (n0 == 0)
        away_part, own_part = zs.at[s, pl.ds(HALF, HALF), lanes], zs.at[s, pl.ds(0, HALF), lanes]

        @pl.when(direct)
        def _():
            to_y(away_part, zin.at[n, s, :, lanes], index)
            pltpu.make_async_copy(own_part, zin.at[n, s, :, lanes], lsem.at[0]).start()

        @pl.when(jnp.logical_not(direct))
        def _():
            to_y(away_part, zy.at[s, :, lanes], index)
            to_z(own_part, zin.at[n, s, :, lanes], 1, zinsem.at[n], 2 * w5)

    def forward_part(s, lanes, index):
        source = zy.at[s, :, lanes]
        pltpu.make_async_copy(source, source, ysem.at[index]).wait()

        @pl.when(jnp.logical_not((n1 != w5) & (n0 == 0)))
        def _():
            to_z(source, zin.at[n, s, :, lanes], 2, zinsem.at[n], 2 * (1 - w5))

    def make_tile(i):
        mixing(i)
        y = column_gate(row_gate(slice(0, N)))
        base = pl.multiple_of(i * 1024, 1024)
        for ct in range(8):
            ytile[pl.ds(base + ct, 2 * HALF, stride=8), :] = y[:, ct * 128:(ct + 1) * 128]

    def spot(i):
        return (i % 2) * 256 + (i // 2) * HALF

    def y_index(i, p):
        return FIRST + (i - 1) * PIECES + p

    def away_piece(i, p, first, count, index):
        r8, j = i % 2, i // 2
        direct = (n1 == w5) & (n0 == r8)
        start = p * PIECE + first
        source = ytile.at[rows8(i * 128 + HALF + start, count)]

        @pl.when(direct)
        def _():
            to_y(source, out.at[rows8(n * 256 + j * HALF + start, count)], index)

        @pl.when(jnp.logical_not(direct))
        def _():
            to_y(source, ybuf.at[rows8(spot(i) + start, count)], index)

    def send_tile(i, last=False):
        r8, j = i % 2, i // 2
        direct = (n1 == w5) & (n0 == r8)
        mine = ytile.at[rows8(i * 128, HALF)]
        where = out.at[rows8(n * 256 + j * HALF, HALF)]
        for p in range(PIECES):
            if last and p == PIECES - 1:
                away_piece(i, p, 0, PIECE - STRAIGHT, y_index(i, p))
            else:
                away_piece(i, p, 0, PIECE, y_index(i, p))
        if last:
            start = HALF - STRAIGHT

            @pl.when(n1 == w5)
            def _():
                away_piece(i, PIECES - 1, PIECE - STRAIGHT, STRAIGHT, y_index(i, PIECES))

            @pl.when(n1 != w5)
            def _():
                pltpu.make_async_remote_copy(
                    src_ref=ytile.at[rows8(i * 128 + HALF + start, STRAIGHT)],
                    dst_ref=out.at[rows8(n * 256 + j * HALF + start, STRAIGHT)],
                    send_sem=ssem.at[3], recv_sem=zsem.at[0],
                    device_id=place_of(1 - w5, 2 * w5 + r8), device_id_type=MESH,
                ).start()

        @pl.when(direct)
        def _():
            pltpu.make_async_copy(mine, where, lsem.at[0]).start()

        @pl.when(jnp.logical_not(direct))
        def _():
            to_z(mine, where, 1, zsem.at[0], 2 * w5 + r8)

    def forward(i, p, first=0, count=PIECE, index=None):
        r8, j = i % 2, i // 2
        start = p * PIECE + first
        source = ybuf.at[rows8(spot(i) + start, count)]
        pltpu.make_async_copy(source, source, ysem.at[y_index(i, p) if index is None else index]).wait()

        @pl.when(jnp.logical_not((n1 != w5) & (n0 == r8)))
        def _():
            target = out.at[rows8(n * 256 + j * HALF + start, count)]
            to_z(source, target, 2, zsem.at[0], 2 * (1 - w5) + r8)

    whole = pl.ds(0, SLAB)
    halves = (pl.ds(0, 128), pl.ds(128, 128))
    rcopy.wait()
    pack(rbv, bcat)
    mixing(0)
    make_part(0, halves[0], half_copy(0))

    @pl.when(n1 == w5)
    def _():
        pl.semaphore_wait(barrier, 4)

    @pl.when(n1 != w5)
    def _():
        pl.semaphore_wait(barrier, 6)

    send_part(0, halves[0], 0)
    make_part(0, halves[1], half_copy(1))
    send_part(0, halves[1], PIECES)
    make_part(1, whole, slab_copy(1))
    send_part(1, whole, 1)
    forward_part(0, halves[0], 0)
    make_part(2, whole, slab_copy(2))
    send_part(2, whole, 2)
    forward_part(0, halves[1], PIECES)
    make_part(3, whole, slab_copy(3))
    send_part(3, whole, 3)
    forward_part(1, whole, 1)
    ccopy.wait()
    pack(cbv, ccat)
    ccat[NNZ * 128:(NNZ + 1) * 128, :] = jnp.zeros((128, 2 * LANES), BF16)

    @pl.loop(0, 64)
    def _(q):
        found = NNZ
        for k in range(NNZ):
            found = found + (cpat[0, k] == q).astype(jnp.int32) * (k - NNZ)
        value = ccat[pl.ds((found & (2 * NNZ - 1)) * 128, 128), :]
        hhi[block(q // 8), block(q % 8)] = value[:, :LANES]
        hlo[block(q // 8), block(q % 8)] = value[:, LANES:]

    forward_part(2, whole, 2)

    @pl.loop(1, TILES - 1)
    def _(i):
        make_tile(i)
        send_tile(i)

        @pl.when(i == 1)
        def _():
            forward_part(3, whole, 3)

        @pl.when(i > 1)
        def _():
            for p in range(PIECES):
                forward(i - 1, p)

    make_tile(TILES - 1)
    send_tile(TILES - 1, last=True)
    for p in range(PIECES):
        forward(TILES - 2, p)
    for p in range(PIECES - 1):
        forward(TILES - 1, p)
    forward(TILES - 1, PIECES - 1, 0, PIECE - STRAIGHT)

    @pl.when(n1 != w5)
    def _():
        forward(TILES - 1, PIECES - 1, PIECE - STRAIGHT, STRAIGHT, y_index(TILES - 1, PIECES))

    def drain(rows, sem):
        ref = ytile.at[pl.ds(0, rows * 8)]
        pltpu.make_async_copy(ref, ref, sem).wait()

    @pl.when(n1 == w5)
    def _():
        drain(256, lsem.at[0])

    @pl.when(n0 == 0)
    def _():
        for q in range(4):
            @pl.when(n != q)
            def _():
                pltpu.make_async_copy(zin.at[q], zin.at[q], zinsem.at[q]).wait()

        @pl.loop(0, 2)
        def _(pair):
            z = jnp.concatenate(
                [
                    jnp.concatenate([zin[2 * pair + h, s] for s in range(PIECES)], axis=1)
                    for h in range(2)
                ],
                axis=0,
            )
            y = column_gate(z)
            for h in range(2):
                base = pl.multiple_of((2 * pair + h) * 2048, 2048)
                for ct in range(8):
                    out[pl.ds(base + ct, HALF, stride=8), :] = y[h * HALF:(h + 1) * HALF, ct * 128:(ct + 1) * 128]

    @pl.when(n1 == w5)
    def _():
        drain(512, ssem.at[0])
        drain(256, ssem.at[1])
        drain(512 - STRAIGHT, ssem.at[2])

    @pl.when(n1 != w5)
    def _():
        drain(512 - STRAIGHT, ssem.at[0])
        drain(512, ssem.at[1])
        drain(256, ssem.at[2])
        drain(STRAIGHT, ssem.at[3])

    @pl.when(n0 == 0)
    def _():
        drain(576, zsem.at[0])

    @pl.when(n0 == 1)
    def _():
        drain(768, zsem.at[0])


def solution(mesh):
    half_wide = mesh.shape["wide"] // 2
    hbm = pl.BlockSpec(memory_space=pltpu.HBM)

    def local(state, col_blocks, row_blocks, col_pattern, row_pattern, qubit_order):
        result = pl.pallas_call(
            functools.partial(exchange, half_wide=half_wide),
            out_shape=jax.ShapeDtypeStruct((8 * N, LANES), F32),
            in_specs=[hbm] * 6,
            out_specs=pl.BlockSpec(memory_space=pltpu.VMEM),
            scratch_shapes=[
                pltpu.SMEM((1, NNZ), jnp.int32),
                pltpu.SMEM((1, NNZ), jnp.int32),
                pltpu.SMEM((1, 10), jnp.int32),
                pltpu.VMEM((NNZ * 128, LANES), F32),
                pltpu.VMEM((NNZ * 128, LANES), F32),
                pltpu.VMEM((PIECES, N, SLAB), F32),
                pltpu.VMEM((N, N), BF16),
                pltpu.VMEM((N, N), BF16),
                pltpu.VMEM((NNZ * 128, 2 * LANES), BF16),
                pltpu.VMEM((2 * NNZ * 128, 2 * LANES), BF16),
                pltpu.VMEM((N, N), BF16),
                pltpu.VMEM((N, N), BF16),
                pltpu.VMEM((2 * HALF, LANES), jnp.int32),
                pltpu.VMEM((256, NNZ * 128), BF16),
                pltpu.VMEM((PIECES, 2 * HALF, SLAB), F32),
                pltpu.VMEM((PIECES, HALF, SLAB), F32),
                pltpu.VMEM((4, PIECES, HALF, SLAB), F32),
                pltpu.VMEM((8 * N, LANES), F32),
                pltpu.VMEM((4 * N, LANES), F32),
                pltpu.SemaphoreType.DMA((FIRST + 5,)),
                pltpu.SemaphoreType.DMA((4,)),
                pltpu.SemaphoreType.DMA((FIRST + (TILES - 1) * PIECES + 1,)),
                pltpu.SemaphoreType.DMA((1,)),
                pltpu.SemaphoreType.DMA((4,)),
                pltpu.SemaphoreType.DMA((1,)),
            ],
            compiler_params=pltpu.CompilerParams(
                collective_id=0, has_side_effects=True, vmem_limit_bytes=48 << 20
            ),
        )(
            *(
                pltpu.with_memory_space_constraint(value, pltpu.HBM)
                for value in (
                    state,
                    col_blocks.reshape(NNZ * 128, LANES),
                    row_blocks.reshape(NNZ * 128, LANES),
                    col_pattern,
                    row_pattern,
                    qubit_order,
                )
            )
        )
        return result.reshape(N, 1, N)

    return jax.shard_map(
        local,
        mesh=mesh,
        in_specs=(P(("wide", "narrow"), None, None), P(), P(), P(), P(), P()),
        out_specs=P(("wide", "narrow"), None, None),
        check_vma=False,
    )
```

```python
import functools

import jax
import jax.numpy as jnp
from jax import lax
from jax.experimental import pallas as pl
from jax.experimental.pallas import tpu as pltpu
from jax.sharding import PartitionSpec as P

MESH = pl.DeviceIdType.MESH
F32, BF16 = jnp.float32, jnp.bfloat16
N = 1024
LANES = 128
NNZ = 16
TILES = 8
HALF = 64
PIECES = 4
PIECE = HALF // PIECES
SLAB = N // PIECES
FIRST = PIECES + 1
STRAIGHT = 6


def split(value):
    hi = value.astype(BF16)
    lo = (value - hi.astype(F32)).astype(BF16)
    return hi, lo


def exchange(
    x_hbm, cb_hbm, rb_hbm, cpat_hbm, rpat_hbm, order_hbm, out,
    cpat, rpat, order, rbv, cbv, xraw, xhi, xlo, bcat, ccat, hhi, hlo, diff, acat,
    zs, zy, zin, ytile, ybuf, insem, ssem, ysem, zsem, zinsem, lsem, go, *, half_wide,
):
    w, n = lax.axis_index("wide"), lax.axis_index("narrow")
    w5, wl = w // half_wide, w % half_wide
    n1, n0 = n // 2, n % 2

    def place_of(a, b):
        return (a * half_wide + wl, b)

    barrier = pltpu.get_barrier_semaphore()
    pl.semaphore_signal(barrier, inc=1, device_id=place_of(1 - w5, n), device_id_type=MESH)

    @pl.when(n != 0)
    def _():
        pl.semaphore_signal(barrier, inc=1, device_id=place_of(w5, 0), device_id_type=MESH)

    def block(k):
        return pl.ds(pl.multiple_of(k * 128, 128), 128)

    def rows8(start, count):
        return pl.ds(pl.multiple_of(start * 8, 8), count * 8)

    def slab_copy(s):
        columns = pl.ds(pl.multiple_of(s * SLAB, SLAB), SLAB)
        return pltpu.make_async_copy(x_hbm.at[:, 0, columns], xraw.at[s], insem.at[s])

    def half_copy(h):
        return pltpu.make_async_copy(
            x_hbm.at[:, 0, pl.ds(h * 128, 128)], xraw.at[0, :, pl.ds(h * 128, 128)], insem.at[PIECES * h]
        )

    small = [
        pltpu.make_async_copy(source, target, insem.at[FIRST + q])
        for q, (source, target) in enumerate(((rpat_hbm, rpat), (cpat_hbm, cpat), (order_hbm, order)))
    ]
    rcopy = pltpu.make_async_copy(rb_hbm, rbv, insem.at[FIRST + 3])
    ccopy = pltpu.make_async_copy(cb_hbm, cbv, insem.at[FIRST + 4])
    for copy in small:
        copy.start()
    rcopy.start()
    for h in range(2):
        half_copy(h).start()
    for s in range(1, PIECES):
        slab_copy(s).start()
    ccopy.start()
    for copy in small:
        copy.wait()

    m = lax.broadcasted_iota(jnp.int32, (2 * HALF, LANES), 0)
    away = m // HALF
    label = (w5 + away - 2 * w5 * away) * (1 << order[0, 9])
    for q in range(6):
        label = label + ((m // (2**q)) % 2) * (1 << order[0, q])
    diff[...] = label - lax.broadcasted_iota(jnp.int32, (2 * HALF, LANES), 1)

    def pack(source, target):
        @pl.loop(0, NNZ)
        def _(k):
            hi, lo = split(source[block(k), :])
            target[block(k), 0:LANES] = hi
            target[block(k), LANES:2 * LANES] = lo

    def mixing(i):
        r8, j = i % 2, i // 2
        base = r8 * (1 << order[0, 8]) + (j % 2) * (1 << order[0, 6]) + (j // 2) * (1 << order[0, 7])
        for k in range(NNZ):
            onehot = (diff[...] == (rpat[0, k] >> 3) * 128 - base).astype(F32).astype(BF16)
            mixed = jnp.dot(onehot, bcat[k * 128:(k + 1) * 128, :], preferred_element_type=F32).astype(BF16)
            acat[0:128, k * 128:(k + 1) * 128] = mixed[:, :LANES]
            acat[128:256, k * 128:(k + 1) * 128] = mixed[:, LANES:]

    def row_gate(columns):
        total = None
        for k in range(0, NNZ, 2):
            left = acat[:, k * 128:(k + 2) * 128]
            first, second = pl.ds((rpat[0, k] & 7) * 128, 128), pl.ds((rpat[0, k + 1] & 7) * 128, 128)
            right = jnp.concatenate([xhi[first, columns], xhi[second, columns]], axis=0)
            both = jnp.dot(left, right, preferred_element_type=F32)
            right = jnp.concatenate([xlo[first, columns], xlo[second, columns]], axis=0)
            term = both[:128] + both[128:] + jnp.dot(left[:128], right, preferred_element_type=F32)
            total = term if total is None else total + term
        return total

    def column_gate(z):
        z_hi, z_lo = split(z)
        both = jnp.concatenate([z_hi, z_lo], axis=0)
        turned = (((1,), (1,)), ((), ()))
        both = lax.dot_general(both, hhi[...], turned, preferred_element_type=F32)
        return both[:128] + both[128:] + lax.dot_general(z_hi, hlo[...], turned, preferred_element_type=F32)

    def to_y(source, target, index):
        pltpu.make_async_remote_copy(
            src_ref=source, dst_ref=target, send_sem=ssem.at[0], recv_sem=ysem.at[index],
            device_id=place_of(1 - w5, n), device_id_type=MESH,
        ).start()

    def to_z(source, target, which, sem, column):
        pltpu.make_async_remote_copy(
            src_ref=source, dst_ref=target, send_sem=ssem.at[which], recv_sem=sem,
            device_id=place_of(w5, column), device_id_type=MESH,
        ).start()

    def make_part(s, lanes, copy):
        columns = pl.ds(pl.multiple_of(s * SLAB + lanes.start, 128), lanes.size)
        copy.wait()

        @pl.loop(0, N // 128)
        def _(b):
            hi, lo = split(xraw[s, block(b), lanes])
            xhi[block(b), columns] = hi
            xlo[block(b), columns] = lo

        zs[s, :, lanes] = row_gate(columns)

    def send_own(s, lanes):
        direct = (n1 == w5) & (n0 == 0)
        own_part = zs.at[s, pl.ds(0, HALF), lanes]

        @pl.when(direct)
        def _():
            pltpu.make_async_copy(own_part, zin.at[n, s, :, lanes], lsem.at[0]).start()

        @pl.when(jnp.logical_not(direct))
        def _():
            to_z(own_part, zin.at[n, s, :, lanes], 1, zinsem.at[n], 2 * w5)

    def send_away(s, lanes, index):
        direct = (n1 == w5) & (n0 == 0)
        away_part = zs.at[s, pl.ds(HALF, HALF), lanes]

        @pl.when(direct)
        def _():
            to_y(away_part, zin.at[n, s, :, lanes], index)

        @pl.when(jnp.logical_not(direct))
        def _():
            to_y(away_part, zy.at[s, :, lanes], index)

    def send_part(s, lanes, index):
        send_away(s, lanes, index)
        send_own(s, lanes)

    def forward_part(s, lanes, index):
        source = zy.at[s, :, lanes]
        pltpu.make_async_copy(source, source, ysem.at[index]).wait()

        @pl.when(jnp.logical_not((n1 != w5) & (n0 == 0)))
        def _():
            to_z(source, zin.at[n, s, :, lanes], 2, zinsem.at[n], 2 * (1 - w5))

    def make_tile(i):
        mixing(i)
        y = column_gate(row_gate(slice(0, N)))
        base = pl.multiple_of(i * 1024, 1024)
        for ct in range(8):
            ytile[pl.ds(base + ct, 2 * HALF, stride=8), :] = y[:, ct * 128:(ct + 1) * 128]

    def spot(i):
        return (i % 2) * 256 + (i // 2) * HALF

    def y_index(i, p):
        return FIRST + (i - 1) * PIECES + p

    def away_piece(i, p, first, count, index):
        r8, j = i % 2, i // 2
        direct = (n1 == w5) & (n0 == r8)
        start = p * PIECE + first
        source = ytile.at[rows8(i * 128 + HALF + start, count)]

        @pl.when(direct)
        def _():
            to_y(source, out.at[rows8(n * 256 + j * HALF + start, count)], index)

        @pl.when(jnp.logical_not(direct))
        def _():
            to_y(source, ybuf.at[rows8(spot(i) + start, count)], index)

    def send_tile(i, last=False):
        r8, j = i % 2, i // 2
        direct = (n1 == w5) & (n0 == r8)
        mine = ytile.at[rows8(i * 128, HALF)]
        where = out.at[rows8(n * 256 + j * HALF, HALF)]
        for p in range(PIECES):
            if last and p == PIECES - 1:
                away_piece(i, p, 0, PIECE - STRAIGHT, y_index(i, p))
            else:
                away_piece(i, p, 0, PIECE, y_index(i, p))
        if last:
            start = HALF - STRAIGHT

            @pl.when(n1 == w5)
            def _():
                away_piece(i, PIECES - 1, PIECE - STRAIGHT, STRAIGHT, y_index(i, PIECES))

            @pl.when(n1 != w5)
            def _():
                pltpu.make_async_remote_copy(
                    src_ref=ytile.at[rows8(i * 128 + HALF + start, STRAIGHT)],
                    dst_ref=out.at[rows8(n * 256 + j * HALF + start, STRAIGHT)],
                    send_sem=ssem.at[3], recv_sem=zsem.at[0],
                    device_id=place_of(1 - w5, 2 * w5 + r8), device_id_type=MESH,
                ).start()

        @pl.when(direct)
        def _():
            pltpu.make_async_copy(mine, where, lsem.at[0]).start()

        @pl.when(jnp.logical_not(direct))
        def _():
            to_z(mine, where, 1, zsem.at[0], 2 * w5 + r8)

    def forward(i, p, first=0, count=PIECE, index=None):
        r8, j = i % 2, i // 2
        start = p * PIECE + first
        source = ybuf.at[rows8(spot(i) + start, count)]
        pltpu.make_async_copy(source, source, ysem.at[y_index(i, p) if index is None else index]).wait()

        @pl.when(jnp.logical_not((n1 != w5) & (n0 == r8)))
        def _():
            target = out.at[rows8(n * 256 + j * HALF + start, count)]
            to_z(source, target, 2, zsem.at[0], 2 * (1 - w5) + r8)

    whole = pl.ds(0, SLAB)
    halves = (pl.ds(0, 128), pl.ds(128, 128))
    rcopy.wait()
    pack(rbv, bcat)
    mixing(0)
    make_part(0, halves[0], half_copy(0))

    @pl.when(n == 0)
    def _():
        pl.semaphore_wait(barrier, 4)
        for j in range(1, 4):
            pl.semaphore_signal(go, inc=1, device_id=place_of(w5, j), device_id_type=MESH)

    @pl.when(n != 0)
    def _():
        pl.semaphore_wait(go, 1)

    send_own(0, halves[0])

    @pl.when(n != 0)
    def _():
        pl.semaphore_wait(barrier, 1)

    send_away(0, halves[0], 0)
    make_part(0, halves[1], half_copy(1))
    send_part(0, halves[1], PIECES)
    make_part(1, whole, slab_copy(1))
    send_part(1, whole, 1)
    forward_part(0, halves[0], 0)
    make_part(2, whole, slab_copy(2))
    send_part(2, whole, 2)
    forward_part(0, halves[1], PIECES)
    make_part(3, whole, slab_copy(3))
    send_part(3, whole, 3)
    forward_part(1, whole, 1)
    ccopy.wait()
    pack(cbv, ccat)
    ccat[NNZ * 128:(NNZ + 1) * 128, :] = jnp.zeros((128, 2 * LANES), BF16)

    @pl.loop(0, 64)
    def _(q):
        found = NNZ
        for k in range(NNZ):
            found = found + (cpat[0, k] == q).astype(jnp.int32) * (k - NNZ)
        value = ccat[pl.ds((found & (2 * NNZ - 1)) * 128, 128), :]
        hhi[block(q // 8), block(q % 8)] = value[:, :LANES]
        hlo[block(q // 8), block(q % 8)] = value[:, LANES:]

    forward_part(2, whole, 2)

    @pl.loop(1, TILES - 1)
    def _(i):
        make_tile(i)
        send_tile(i)

        @pl.when(i == 1)
        def _():
            forward_part(3, whole, 3)

        @pl.when(i > 1)
        def _():
            for p in range(PIECES):
                forward(i - 1, p)

    make_tile(TILES - 1)
    send_tile(TILES - 1, last=True)
    for p in range(PIECES):
        forward(TILES - 2, p)
    for p in range(PIECES - 1):
        forward(TILES - 1, p)
    forward(TILES - 1, PIECES - 1, 0, PIECE - STRAIGHT)

    @pl.when(n1 != w5)
    def _():
        forward(TILES - 1, PIECES - 1, PIECE - STRAIGHT, STRAIGHT, y_index(TILES - 1, PIECES))

    def drain(rows, sem):
        ref = ytile.at[pl.ds(0, rows * 8)]
        pltpu.make_async_copy(ref, ref, sem).wait()

    @pl.when(n1 == w5)
    def _():
        drain(256, lsem.at[0])

    @pl.when(n0 == 0)
    def _():
        for q in range(4):
            @pl.when(n != q)
            def _():
                pltpu.make_async_copy(zin.at[q], zin.at[q], zinsem.at[q]).wait()

        @pl.loop(0, 2)
        def _(pair):
            z = jnp.concatenate(
                [
                    jnp.concatenate([zin[2 * pair + h, s] for s in range(PIECES)], axis=1)
                    for h in range(2)
                ],
                axis=0,
            )
            y = column_gate(z)
            for h in range(2):
                base = pl.multiple_of((2 * pair + h) * 2048, 2048)
                for ct in range(8):
                    out[pl.ds(base + ct, HALF, stride=8), :] = y[h * HALF:(h + 1) * HALF, ct * 128:(ct + 1) * 128]

    @pl.when(n1 == w5)
    def _():
        drain(512, ssem.at[0])
        drain(256, ssem.at[1])
        drain(512 - STRAIGHT, ssem.at[2])

    @pl.when(n1 != w5)
    def _():
        drain(512 - STRAIGHT, ssem.at[0])
        drain(512, ssem.at[1])
        drain(256, ssem.at[2])
        drain(STRAIGHT, ssem.at[3])

    @pl.when(n0 == 0)
    def _():
        drain(576, zsem.at[0])

    @pl.when(n0 == 1)
    def _():
        drain(768, zsem.at[0])


def solution(mesh):
    half_wide = mesh.shape["wide"] // 2
    hbm = pl.BlockSpec(memory_space=pltpu.HBM)

    def local(state, col_blocks, row_blocks, col_pattern, row_pattern, qubit_order):
        result = pl.pallas_call(
            functools.partial(exchange, half_wide=half_wide),
            out_shape=jax.ShapeDtypeStruct((8 * N, LANES), F32),
            in_specs=[hbm] * 6,
            out_specs=pl.BlockSpec(memory_space=pltpu.VMEM),
            scratch_shapes=[
                pltpu.SMEM((1, NNZ), jnp.int32),
                pltpu.SMEM((1, NNZ), jnp.int32),
                pltpu.SMEM((1, 10), jnp.int32),
                pltpu.VMEM((NNZ * 128, LANES), F32),
                pltpu.VMEM((NNZ * 128, LANES), F32),
                pltpu.VMEM((PIECES, N, SLAB), F32),
                pltpu.VMEM((N, N), BF16),
                pltpu.VMEM((N, N), BF16),
                pltpu.VMEM((NNZ * 128, 2 * LANES), BF16),
                pltpu.VMEM((2 * NNZ * 128, 2 * LANES), BF16),
                pltpu.VMEM((N, N), BF16),
                pltpu.VMEM((N, N), BF16),
                pltpu.VMEM((2 * HALF, LANES), jnp.int32),
                pltpu.VMEM((256, NNZ * 128), BF16),
                pltpu.VMEM((PIECES, 2 * HALF, SLAB), F32),
                pltpu.VMEM((PIECES, HALF, SLAB), F32),
                pltpu.VMEM((4, PIECES, HALF, SLAB), F32),
                pltpu.VMEM((8 * N, LANES), F32),
                pltpu.VMEM((4 * N, LANES), F32),
                pltpu.SemaphoreType.DMA((FIRST + 5,)),
                pltpu.SemaphoreType.DMA((4,)),
                pltpu.SemaphoreType.DMA((FIRST + (TILES - 1) * PIECES + 1,)),
                pltpu.SemaphoreType.DMA((1,)),
                pltpu.SemaphoreType.DMA((4,)),
                pltpu.SemaphoreType.DMA((1,)),
                pltpu.SemaphoreType.REGULAR,
            ],
            compiler_params=pltpu.CompilerParams(
                collective_id=0, has_side_effects=True, vmem_limit_bytes=48 << 20
            ),
        )(
            *(
                pltpu.with_memory_space_constraint(value, pltpu.HBM)
                for value in (
                    state,
                    col_blocks.reshape(NNZ * 128, LANES),
                    row_blocks.reshape(NNZ * 128, LANES),
                    col_pattern,
                    row_pattern,
                    qubit_order,
                )
            )
        )
        return result.reshape(N, 1, N)

    return jax.shard_map(
        local,
        mesh=mesh,
        in_specs=(P(("wide", "narrow"), None, None), P(), P(), P(), P(), P()),
        out_specs=P(("wide", "narrow"), None, None),
        check_vma=False,
    )
```

```python
import functools

import jax
import jax.numpy as jnp
from jax import lax
from jax.experimental import pallas as pl
from jax.experimental.pallas import tpu as pltpu
from jax.sharding import PartitionSpec as P

MESH = pl.DeviceIdType.MESH
F32, BF16 = jnp.float32, jnp.bfloat16
N = 1024
LANES = 128
NNZ = 16
TILES = 8
HALF = 64
PIECES = 4
PIECE = HALF // PIECES
SLAB = N // PIECES
FIRST = PIECES + 1
STRAIGHT = 6


def split(value):
    hi = value.astype(BF16)
    lo = (value - hi.astype(F32)).astype(BF16)
    return hi, lo


def exchange(
    x_hbm, cb_hbm, rb_hbm, cpat_hbm, rpat_hbm, order_hbm, out,
    cpat, rpat, order, rbv, cbv, xraw, xhi, xlo, bcat, ccat, hhi, hlo, diff, acat,
    zs, zy, zin, ytile, ybuf, insem, ssem, ysem, zsem, zinsem, lsem, *, half_wide,
):
    w, n = lax.axis_index("wide"), lax.axis_index("narrow")
    w5, wl = w // half_wide, w % half_wide
    n1, n0 = n // 2, n % 2

    def place_of(a, b):
        return (a * half_wide + wl, b)

    barrier = pltpu.get_barrier_semaphore()
    pl.semaphore_signal(barrier, inc=1, device_id=place_of(1 - w5, n), device_id_type=MESH)
    for j in range(1, 4):
        pl.semaphore_signal(barrier, inc=1, device_id=place_of(w5, lax.rem(n + j, 4)), device_id_type=MESH)

    @pl.when(n1 != w5)
    def _():
        for j in range(2):
            pl.semaphore_signal(barrier, inc=1, device_id=place_of(1 - w5, 2 * w5 + j), device_id_type=MESH)

    def block(k):
        return pl.ds(pl.multiple_of(k * 128, 128), 128)

    def rows8(start, count):
        return pl.ds(pl.multiple_of(start * 8, 8), count * 8)

    def slab_copy(s):
        columns = pl.ds(pl.multiple_of(s * SLAB, SLAB), SLAB)
        return pltpu.make_async_copy(x_hbm.at[:, 0, columns], xraw.at[s], insem.at[s])

    def half_copy(h):
        return pltpu.make_async_copy(
            x_hbm.at[:, 0, pl.ds(h * 128, 128)], xraw.at[0, :, pl.ds(h * 128, 128)], insem.at[PIECES * h]
        )

    small = [
        pltpu.make_async_copy(source, target, insem.at[FIRST + q])
        for q, (source, target) in enumerate(((rpat_hbm, rpat), (cpat_hbm, cpat), (order_hbm, order)))
    ]
    rcopy = pltpu.make_async_copy(rb_hbm, rbv, insem.at[FIRST + 3])
    ccopy = pltpu.make_async_copy(cb_hbm, cbv, insem.at[FIRST + 4])
    for copy in small:
        copy.start()
    rcopy.start()
    for h in range(2):
        half_copy(h).start()
    for s in range(1, PIECES):
        slab_copy(s).start()
    ccopy.start()
    for copy in small:
        copy.wait()

    m = lax.broadcasted_iota(jnp.int32, (2 * HALF, LANES), 0)
    away = m // HALF
    label = (w5 + away - 2 * w5 * away) * (1 << order[0, 9])
    for q in range(6):
        label = label + ((m // (2**q)) % 2) * (1 << order[0, q])
    diff[...] = label - lax.broadcasted_iota(jnp.int32, (2 * HALF, LANES), 1)

    def pack(source, target):
        @pl.loop(0, NNZ)
        def _(k):
            hi, lo = split(source[block(k), :])
            target[block(k), 0:LANES] = hi
            target[block(k), LANES:2 * LANES] = lo

    def mixing(i):
        r8, j = i % 2, i // 2
        base = r8 * (1 << order[0, 8]) + (j % 2) * (1 << order[0, 6]) + (j // 2) * (1 << order[0, 7])
        for k in range(NNZ):
            onehot = (diff[...] == (rpat[0, k] >> 3) * 128 - base).astype(F32).astype(BF16)
            mixed = jnp.dot(onehot, bcat[k * 128:(k + 1) * 128, :], preferred_element_type=F32).astype(BF16)
            acat[0:128, k * 128:(k + 1) * 128] = mixed[:, :LANES]
            acat[128:256, k * 128:(k + 1) * 128] = mixed[:, LANES:]

    def row_gate(columns):
        total = None
        for k in range(0, NNZ, 2):
            left = acat[:, k * 128:(k + 2) * 128]
            first, second = pl.ds((rpat[0, k] & 7) * 128, 128), pl.ds((rpat[0, k + 1] & 7) * 128, 128)
            right = jnp.concatenate([xhi[first, columns], xhi[second, columns]], axis=0)
            both = jnp.dot(left, right, preferred_element_type=F32)
            right = jnp.concatenate([xlo[first, columns], xlo[second, columns]], axis=0)
            term = both[:128] + both[128:] + jnp.dot(left[:128], right, preferred_element_type=F32)
            total = term if total is None else total + term
        return total

    def column_gate(z):
        z_hi, z_lo = split(z)
        both = jnp.concatenate([z_hi, z_lo], axis=0)
        turned = (((1,), (1,)), ((), ()))
        both = lax.dot_general(both, hhi[...], turned, preferred_element_type=F32)
        return both[:128] + both[128:] + lax.dot_general(z_hi, hlo[...], turned, preferred_element_type=F32)

    def to_y(source, target, index):
        pltpu.make_async_remote_copy(
            src_ref=source, dst_ref=target, send_sem=ssem.at[0], recv_sem=ysem.at[index],
            device_id=place_of(1 - w5, n), device_id_type=MESH,
        ).start()

    def to_z(source, target, which, sem, column):
        pltpu.make_async_remote_copy(
            src_ref=source, dst_ref=target, send_sem=ssem.at[which], recv_sem=sem,
            device_id=place_of(w5, column), device_id_type=MESH,
        ).start()

    def make_part(s, lanes, copy):
        columns = pl.ds(pl.multiple_of(s * SLAB + lanes.start, 128), lanes.size)
        copy.wait()

        @pl.loop(0, N // 128)
        def _(b):
            hi, lo = split(xraw[s, block(b), lanes])
            xhi[block(b), columns] = hi
            xlo[block(b), columns] = lo

        zs[0, s, :, lanes] = row_gate(columns)

    def send_part(t, s, lanes, index):
        direct = (n1 == w5) & (n0 == t)
        away_part, own_part = zs.at[t, s, pl.ds(HALF, HALF), lanes], zs.at[t, s, pl.ds(0, HALF), lanes]
        target = zin.at[n, s, :, lanes]

        @pl.when(direct)
        def _():
            to_y(away_part, target, index)
            pltpu.make_async_copy(own_part, target, lsem.at[0]).start()

        @pl.when(jnp.logical_not(direct))
        def _():
            to_y(away_part, zy.at[t, s, :, lanes], index)
            to_z(own_part, target, 1, zinsem.at[n], 2 * w5 + t)

    def forward_part(t, s, lanes, index):
        source = zy.at[t, s, :, lanes]
        pltpu.make_async_copy(source, source, ysem.at[index]).wait()

        @pl.when(jnp.logical_not((n1 != w5) & (n0 == t)))
        def _():
            to_z(source, zin.at[n, s, :, lanes], 2, zinsem.at[n], 2 * (1 - w5) + t)

    def make_tile(i):
        mixing(i)
        y = column_gate(row_gate(slice(0, N)))
        base = pl.multiple_of(i * 1024, 1024)
        for ct in range(8):
            ytile[pl.ds(base + ct, 2 * HALF, stride=8), :] = y[:, ct * 128:(ct + 1) * 128]

    def spot(i):
        return (i % 2) * 256 + (i // 2) * HALF

    def y_index(i, p):
        return FIRST + (i - 1) * PIECES + p

    def away_piece(i, p, first, count, index):
        r8, j = i % 2, i // 2
        direct = (n1 == w5) & (n0 == r8)
        start = p * PIECE + first
        source = ytile.at[rows8(i * 128 + HALF + start, count)]

        @pl.when(direct)
        def _():
            to_y(source, out.at[rows8(n * 256 + j * HALF + start, count)], index)

        @pl.when(jnp.logical_not(direct))
        def _():
            to_y(source, ybuf.at[rows8(spot(i) + start, count)], index)

    def send_tile(i, last=False):
        r8, j = i % 2, i // 2
        direct = (n1 == w5) & (n0 == r8)
        mine = ytile.at[rows8(i * 128, HALF)]
        where = out.at[rows8(n * 256 + j * HALF, HALF)]
        for p in range(PIECES):
            if last and p == PIECES - 1:
                away_piece(i, p, 0, PIECE - STRAIGHT, y_index(i, p))
            else:
                away_piece(i, p, 0, PIECE, y_index(i, p))
        if last:
            start = HALF - STRAIGHT

            @pl.when(n1 == w5)
            def _():
                away_piece(i, PIECES - 1, PIECE - STRAIGHT, STRAIGHT, y_index(i, PIECES))

            @pl.when(n1 != w5)
            def _():
                pltpu.make_async_remote_copy(
                    src_ref=ytile.at[rows8(i * 128 + HALF + start, STRAIGHT)],
                    dst_ref=out.at[rows8(n * 256 + j * HALF + start, STRAIGHT)],
                    send_sem=ssem.at[3], recv_sem=zsem.at[0],
                    device_id=place_of(1 - w5, 2 * w5 + r8), device_id_type=MESH,
                ).start()

        @pl.when(direct)
        def _():
            pltpu.make_async_copy(mine, where, lsem.at[0]).start()

        @pl.when(jnp.logical_not(direct))
        def _():
            to_z(mine, where, 1, zsem.at[0], 2 * w5 + r8)

    def forward(i, p, first=0, count=PIECE, index=None):
        r8, j = i % 2, i // 2
        start = p * PIECE + first
        source = ybuf.at[rows8(spot(i) + start, count)]
        pltpu.make_async_copy(source, source, ysem.at[y_index(i, p) if index is None else index]).wait()

        @pl.when(jnp.logical_not((n1 != w5) & (n0 == r8)))
        def _():
            target = out.at[rows8(n * 256 + j * HALF + start, count)]
            to_z(source, target, 2, zsem.at[0], 2 * (1 - w5) + r8)

    whole = pl.ds(0, SLAB)
    halves = (pl.ds(0, 128), pl.ds(128, 128))
    rcopy.wait()
    pack(rbv, bcat)
    mixing(0)
    make_part(0, halves[0], half_copy(0))

    @pl.when(n1 == w5)
    def _():
        pl.semaphore_wait(barrier, 4)

    @pl.when(n1 != w5)
    def _():
        pl.semaphore_wait(barrier, 6)

    send_part(0, 0, halves[0], 0)
    make_part(0, halves[1], half_copy(1))
    send_part(0, 0, halves[1], PIECES)
    make_part(1, whole, slab_copy(1))
    send_part(0, 1, whole, 1)
    forward_part(0, 0, halves[0], 0)
    make_part(2, whole, slab_copy(2))
    send_part(0, 2, whole, 2)
    forward_part(0, 0, halves[1], PIECES)
    make_part(3, whole, slab_copy(3))
    send_part(0, 3, whole, 3)
    mixing(1)

    @pl.loop(0, 2)
    def _(half):
        forward_part(0, 1 + half, whole, 1 + half)
        for q in range(2):
            s = half * 2 + q
            zs[1, s] = row_gate(pl.ds(pl.multiple_of(s * SLAB, SLAB), SLAB))
            send_part(1, s, whole, y_index(1, s))

    ccopy.wait()
    pack(cbv, ccat)
    ccat[NNZ * 128:(NNZ + 1) * 128, :] = jnp.zeros((128, 2 * LANES), BF16)

    @pl.loop(0, 64)
    def _(q):
        found = NNZ
        for k in range(NNZ):
            found = found + (cpat[0, k] == q).astype(jnp.int32) * (k - NNZ)
        value = ccat[pl.ds((found & (2 * NNZ - 1)) * 128, 128), :]
        hhi[block(q // 8), block(q % 8)] = value[:, :LANES]
        hlo[block(q // 8), block(q % 8)] = value[:, LANES:]

    forward_part(0, 3, whole, 3)

    @pl.loop(2, TILES - 1)
    def _(i):
        make_tile(i)
        send_tile(i)

        @pl.when(i == 2)
        def _():
            for s in range(PIECES):
                forward_part(1, s, whole, y_index(1, s))

        @pl.when(i > 2)
        def _():
            for p in range(PIECES):
                forward(i - 1, p)

    make_tile(TILES - 1)
    send_tile(TILES - 1, last=True)
    for p in range(PIECES):
        forward(TILES - 2, p)
    for p in range(PIECES - 1):
        forward(TILES - 1, p)
    forward(TILES - 1, PIECES - 1, 0, PIECE - STRAIGHT)

    @pl.when(n1 != w5)
    def _():
        forward(TILES - 1, PIECES - 1, PIECE - STRAIGHT, STRAIGHT, y_index(TILES - 1, PIECES))

    def drain(rows, sem):
        ref = ytile.at[pl.ds(0, rows * 8)]
        pltpu.make_async_copy(ref, ref, sem).wait()

    @pl.when(n1 == w5)
    def _():
        drain(256, lsem.at[0])

    for q in range(4):
        @pl.when(n != q)
        def _():
            pltpu.make_async_copy(zin.at[q], zin.at[q], zinsem.at[q]).wait()

    @pl.loop(0, 2)
    def _(pair):
        z = jnp.concatenate(
            [
                jnp.concatenate([zin[2 * pair + h, s] for s in range(PIECES)], axis=1)
                for h in range(2)
            ],
            axis=0,
        )
        y = column_gate(z)
        for h in range(2):
            base = pl.multiple_of((2 * pair + h) * 2048, 2048)
            for ct in range(8):
                out[pl.ds(base + ct, HALF, stride=8), :] = y[h * HALF:(h + 1) * HALF, ct * 128:(ct + 1) * 128]

    @pl.when(n1 == w5)
    def _():
        drain(512, ssem.at[0])
        drain(256, ssem.at[1])
        drain(512 - STRAIGHT, ssem.at[2])

    @pl.when(n1 != w5)
    def _():
        drain(512 - STRAIGHT, ssem.at[0])
        drain(512, ssem.at[1])
        drain(256, ssem.at[2])
        drain(STRAIGHT, ssem.at[3])

    drain(576, zsem.at[0])


def solution(mesh):
    half_wide = mesh.shape["wide"] // 2
    hbm = pl.BlockSpec(memory_space=pltpu.HBM)

    def local(state, col_blocks, row_blocks, col_pattern, row_pattern, qubit_order):
        result = pl.pallas_call(
            functools.partial(exchange, half_wide=half_wide),
            out_shape=jax.ShapeDtypeStruct((8 * N, LANES), F32),
            in_specs=[hbm] * 6,
            out_specs=pl.BlockSpec(memory_space=pltpu.VMEM),
            scratch_shapes=[
                pltpu.SMEM((1, NNZ), jnp.int32),
                pltpu.SMEM((1, NNZ), jnp.int32),
                pltpu.SMEM((1, 10), jnp.int32),
                pltpu.VMEM((NNZ * 128, LANES), F32),
                pltpu.VMEM((NNZ * 128, LANES), F32),
                pltpu.VMEM((PIECES, N, SLAB), F32),
                pltpu.VMEM((N, N), BF16),
                pltpu.VMEM((N, N), BF16),
                pltpu.VMEM((NNZ * 128, 2 * LANES), BF16),
                pltpu.VMEM((2 * NNZ * 128, 2 * LANES), BF16),
                pltpu.VMEM((N, N), BF16),
                pltpu.VMEM((N, N), BF16),
                pltpu.VMEM((2 * HALF, LANES), jnp.int32),
                pltpu.VMEM((256, NNZ * 128), BF16),
                pltpu.VMEM((2, PIECES, 2 * HALF, SLAB), F32),
                pltpu.VMEM((2, PIECES, HALF, SLAB), F32),
                pltpu.VMEM((4, PIECES, HALF, SLAB), F32),
                pltpu.VMEM((8 * N, LANES), F32),
                pltpu.VMEM((4 * N, LANES), F32),
                pltpu.SemaphoreType.DMA((FIRST + 5,)),
                pltpu.SemaphoreType.DMA((4,)),
                pltpu.SemaphoreType.DMA((FIRST + (TILES - 1) * PIECES + 1,)),
                pltpu.SemaphoreType.DMA((1,)),
                pltpu.SemaphoreType.DMA((4,)),
                pltpu.SemaphoreType.DMA((1,)),
            ],
            compiler_params=pltpu.CompilerParams(
                collective_id=0, has_side_effects=True, vmem_limit_bytes=48 << 20
            ),
        )(
            *(
                pltpu.with_memory_space_constraint(value, pltpu.HBM)
                for value in (
                    state,
                    col_blocks.reshape(NNZ * 128, LANES),
                    row_blocks.reshape(NNZ * 128, LANES),
                    col_pattern,
                    row_pattern,
                    qubit_order,
                )
            )
        )
        return result.reshape(N, 1, N)

    return jax.shard_map(
        local,
        mesh=mesh,
        in_specs=(P(("wide", "narrow"), None, None), P(), P(), P(), P(), P()),
        out_specs=P(("wide", "narrow"), None, None),
        check_vma=False,
    )
```

```python
import functools

import jax
import jax.numpy as jnp
from jax import lax
from jax.experimental import pallas as pl
from jax.experimental.pallas import tpu as pltpu
from jax.sharding import PartitionSpec as P

MESH = pl.DeviceIdType.MESH
F32, BF16 = jnp.float32, jnp.bfloat16
N = 1024
LANES = 128
NNZ = 16
TILES = 8
HALF = 64
PIECES = 4
PIECE = HALF // PIECES
SLAB = N // PIECES
FIRST = PIECES + 1
STRAIGHT = 6


def split(value):
    hi = value.astype(BF16)
    lo = (value - hi.astype(F32)).astype(BF16)
    return hi, lo


def exchange(
    x_hbm, cb_hbm, rb_hbm, cpat_hbm, rpat_hbm, order_hbm, out,
    cpat, rpat, order, rbv, cbv, xraw, xhi, xlo, bcat, ccat, hhi, hlo, diff, acat,
    zs, zy, zin, ytile, ybuf, insem, ssem, ysem, zsem, zinsem, lsem, *, half_wide,
):
    w, n = lax.axis_index("wide"), lax.axis_index("narrow")
    w5, wl = w // half_wide, w % half_wide
    n1, n0 = n // 2, n % 2

    def place_of(a, b):
        return (a * half_wide + wl, b)

    barrier = pltpu.get_barrier_semaphore()
    pl.semaphore_signal(barrier, inc=1, device_id=place_of(1 - w5, n), device_id_type=MESH)
    for j in range(1, 4):
        pl.semaphore_signal(barrier, inc=1, device_id=place_of(w5, lax.rem(n + j, 4)), device_id_type=MESH)

    @pl.when(n1 != w5)
    def _():
        for j in range(2):
            pl.semaphore_signal(barrier, inc=1, device_id=place_of(1 - w5, 2 * w5 + j), device_id_type=MESH)

    def block(k):
        return pl.ds(pl.multiple_of(k * 128, 128), 128)

    def rows8(start, count):
        return pl.ds(pl.multiple_of(start * 8, 8), count * 8)

    def slab_copy(s):
        columns = pl.ds(pl.multiple_of(s * SLAB, SLAB), SLAB)
        return pltpu.make_async_copy(x_hbm.at[:, 0, columns], xraw.at[s], insem.at[s])

    def half_copy(h):
        return pltpu.make_async_copy(
            x_hbm.at[:, 0, pl.ds(h * 128, 128)], xraw.at[0, :, pl.ds(h * 128, 128)], insem.at[PIECES * h]
        )

    small = [
        pltpu.make_async_copy(source, target, insem.at[FIRST + q])
        for q, (source, target) in enumerate(((rpat_hbm, rpat), (cpat_hbm, cpat), (order_hbm, order)))
    ]
    rcopy = pltpu.make_async_copy(rb_hbm, rbv, insem.at[FIRST + 3])
    ccopy = pltpu.make_async_copy(cb_hbm, cbv, insem.at[FIRST + 4])
    for copy in small:
        copy.start()
    rcopy.start()
    for h in range(2):
        half_copy(h).start()
    for s in range(1, PIECES):
        slab_copy(s).start()
    ccopy.start()
    for copy in small:
        copy.wait()

    m = lax.broadcasted_iota(jnp.int32, (2 * HALF, LANES), 0)
    away = m // HALF
    label = (w5 + away - 2 * w5 * away) * (1 << order[0, 9])
    for q in range(6):
        label = label + ((m // (2**q)) % 2) * (1 << order[0, q])
    diff[...] = label - lax.broadcasted_iota(jnp.int32, (2 * HALF, LANES), 1)

    def pack(source, target):
        @pl.loop(0, NNZ)
        def _(k):
            hi, lo = split(source[block(k), :])
            target[block(k), 0:LANES] = hi
            target[block(k), LANES:2 * LANES] = lo

    def mixing(i):
        r8, j = i % 2, i // 2
        base = r8 * (1 << order[0, 8]) + (j % 2) * (1 << order[0, 6]) + (j // 2) * (1 << order[0, 7])
        for k in range(NNZ):
            onehot = (diff[...] == (rpat[0, k] >> 3) * 128 - base).astype(F32).astype(BF16)
            mixed = jnp.dot(onehot, bcat[k * 128:(k + 1) * 128, :], preferred_element_type=F32).astype(BF16)
            acat[0:128, k * 128:(k + 1) * 128] = mixed[:, :LANES]
            acat[128:256, k * 128:(k + 1) * 128] = mixed[:, LANES:]

    def row_gate(columns):
        total = None
        for k in range(0, NNZ, 2):
            left = acat[:, k * 128:(k + 2) * 128]
            first, second = pl.ds((rpat[0, k] & 7) * 128, 128), pl.ds((rpat[0, k + 1] & 7) * 128, 128)
            right = jnp.concatenate([xhi[first, columns], xhi[second, columns]], axis=0)
            both = jnp.dot(left, right, preferred_element_type=F32)
            right = jnp.concatenate([xlo[first, columns], xlo[second, columns]], axis=0)
            term = both[:128] + both[128:] + jnp.dot(left[:128], right, preferred_element_type=F32)
            total = term if total is None else total + term
        return total

    def column_gate(z):
        z_hi, z_lo = split(z)
        both = jnp.concatenate([z_hi, z_lo], axis=0)
        turned = (((1,), (1,)), ((), ()))
        both = lax.dot_general(both, hhi[...], turned, preferred_element_type=F32)
        return both[:128] + both[128:] + lax.dot_general(z_hi, hlo[...], turned, preferred_element_type=F32)

    def to_y(source, target, index):
        pltpu.make_async_remote_copy(
            src_ref=source, dst_ref=target, send_sem=ssem.at[0], recv_sem=ysem.at[index],
            device_id=place_of(1 - w5, n), device_id_type=MESH,
        ).start()

    def to_z(source, target, which, sem, column):
        pltpu.make_async_remote_copy(
            src_ref=source, dst_ref=target, send_sem=ssem.at[which], recv_sem=sem,
            device_id=place_of(w5, column), device_id_type=MESH,
        ).start()

    def make_part(s, lanes, copy):
        columns = pl.ds(pl.multiple_of(s * SLAB + lanes.start, 128), lanes.size)
        copy.wait()

        @pl.loop(0, N // 128)
        def _(b):
            hi, lo = split(xraw[s, block(b), lanes])
            xhi[block(b), columns] = hi
            xlo[block(b), columns] = lo

        zs[s, :, lanes] = row_gate(columns)

    def send_part(s, lanes, index):
        direct = (n1 == w5) & (n0 == 0)
        away_part, own_part = zs.at[s, pl.ds(HALF, HALF), lanes], zs.at[s, pl.ds(0, HALF), lanes]

        @pl.when(direct)
        def _():
            to_y(away_part, zin.at[n, s, :, lanes], index)
            pltpu.make_async_copy(own_part, zin.at[n, s, :, lanes], lsem.at[0]).start()

        @pl.when(jnp.logical_not(direct))
        def _():
            to_y(away_part, zy.at[s, :, lanes], index)
            to_z(own_part, zin.at[n, s, :, lanes], 1, zinsem.at[n], 2 * w5)

    def forward_part(s, lanes, index):
        source = zy.at[s, :, lanes]
        pltpu.make_async_copy(source, source, ysem.at[index]).wait()

        @pl.when(jnp.logical_not((n1 != w5) & (n0 == 0)))
        def _():
            to_z(source, zin.at[n, s, :, lanes], 2, zinsem.at[n], 2 * (1 - w5))

    def make_tile(i):
        mixing(i)
        y = column_gate(row_gate(slice(0, N)))
        base = pl.multiple_of(i * 1024, 1024)
        for ct in range(8):
            ytile[pl.ds(base + ct, 2 * HALF, stride=8), :] = y[:, ct * 128:(ct + 1) * 128]

    def spot(i):
        return (i % 2) * 256 + (i // 2) * HALF

    def y_index(i, p):
        return FIRST + (i - 1) * PIECES + p

    def away_piece(i, p, first, count, index):
        r8, j = i % 2, i // 2
        direct = (n1 == w5) & (n0 == r8)
        start = p * PIECE + first
        source = ytile.at[rows8(i * 128 + HALF + start, count)]

        @pl.when(direct)
        def _():
            to_y(source, out.at[rows8(n * 256 + j * HALF + start, count)], index)

        @pl.when(jnp.logical_not(direct))
        def _():
            to_y(source, ybuf.at[rows8(spot(i) + start, count)], index)

    last_a = (PIECES - 1, 0, PIECE - STRAIGHT)
    last_b = (PIECES - 1, PIECE - STRAIGHT, STRAIGHT)
    a_straight = (n1 != w5) & (w5 == 1)
    a_skipped = (n1 == w5) & (w5 == 0)

    def straight(i, piece):
        r8, j = i % 2, i // 2
        p, first, count = piece
        start = p * PIECE + first
        pltpu.make_async_remote_copy(
            src_ref=ytile.at[rows8(i * 128 + HALF + start, count)],
            dst_ref=out.at[rows8(n * 256 + j * HALF + start, count)],
            send_sem=ssem.at[3], recv_sem=zsem.at[0],
            device_id=place_of(1 - w5, 2 * w5 + r8), device_id_type=MESH,
        ).start()

    def send_tile(i, last=False):
        r8, j = i % 2, i // 2
        direct = (n1 == w5) & (n0 == r8)
        mine = ytile.at[rows8(i * 128, HALF)]
        where = out.at[rows8(n * 256 + j * HALF, HALF)]
        for p in range(PIECES - last):
            away_piece(i, p, 0, PIECE, y_index(i, p))
        if last:
            @pl.when(a_straight)
            def _():
                straight(i, last_a)

            @pl.when(jnp.logical_not(a_straight))
            def _():
                away_piece(i, *last_a, y_index(i, PIECES - 1))

            @pl.when(n1 != w5)
            def _():
                straight(i, last_b)

            @pl.when(n1 == w5)
            def _():
                away_piece(i, *last_b, y_index(i, PIECES))

        @pl.when(direct)
        def _():
            pltpu.make_async_copy(mine, where, lsem.at[0]).start()

        @pl.when(jnp.logical_not(direct))
        def _():
            to_z(mine, where, 1, zsem.at[0], 2 * w5 + r8)

    def forward(i, p, first=0, count=PIECE, index=None):
        r8, j = i % 2, i // 2
        start = p * PIECE + first
        source = ybuf.at[rows8(spot(i) + start, count)]
        pltpu.make_async_copy(source, source, ysem.at[y_index(i, p) if index is None else index]).wait()

        @pl.when(jnp.logical_not((n1 != w5) & (n0 == r8)))
        def _():
            target = out.at[rows8(n * 256 + j * HALF + start, count)]
            to_z(source, target, 2, zsem.at[0], 2 * (1 - w5) + r8)

    whole = pl.ds(0, SLAB)
    halves = (pl.ds(0, 128), pl.ds(128, 128))
    rcopy.wait()
    pack(rbv, bcat)
    mixing(0)
    make_part(0, halves[0], half_copy(0))

    @pl.when(n1 == w5)
    def _():
        pl.semaphore_wait(barrier, 4)

    @pl.when(n1 != w5)
    def _():
        pl.semaphore_wait(barrier, 6)

    send_part(0, halves[0], 0)
    make_part(0, halves[1], half_copy(1))
    send_part(0, halves[1], PIECES)
    make_part(1, whole, slab_copy(1))
    send_part(1, whole, 1)
    forward_part(0, halves[0], 0)
    make_part(2, whole, slab_copy(2))
    send_part(2, whole, 2)
    forward_part(0, halves[1], PIECES)
    make_part(3, whole, slab_copy(3))
    send_part(3, whole, 3)
    forward_part(1, whole, 1)
    ccopy.wait()
    pack(cbv, ccat)
    ccat[NNZ * 128:(NNZ + 1) * 128, :] = jnp.zeros((128, 2 * LANES), BF16)

    @pl.loop(0, 64)
    def _(q):
        found = NNZ
        for k in range(NNZ):
            found = found + (cpat[0, k] == q).astype(jnp.int32) * (k - NNZ)
        value = ccat[pl.ds((found & (2 * NNZ - 1)) * 128, 128), :]
        hhi[block(q // 8), block(q % 8)] = value[:, :LANES]
        hlo[block(q // 8), block(q % 8)] = value[:, LANES:]

    forward_part(2, whole, 2)

    @pl.loop(1, TILES - 1)
    def _(i):
        make_tile(i)
        send_tile(i)

        @pl.when(i == 1)
        def _():
            forward_part(3, whole, 3)

        @pl.when(i > 1)
        def _():
            for p in range(PIECES):
                forward(i - 1, p)

    make_tile(TILES - 1)
    send_tile(TILES - 1, last=True)
    for p in range(PIECES):
        forward(TILES - 2, p)
    for p in range(PIECES - 1):
        forward(TILES - 1, p)

    @pl.when(jnp.logical_not(a_skipped))
    def _():
        forward(TILES - 1, *last_a)

    @pl.when(n1 != w5)
    def _():
        forward(TILES - 1, *last_b, y_index(TILES - 1, PIECES))

    def drain(rows, sem):
        ref = ytile.at[pl.ds(0, rows * 8)]
        pltpu.make_async_copy(ref, ref, sem).wait()

    @pl.when(n1 == w5)
    def _():
        drain(256, lsem.at[0])

    @pl.when(n0 == 0)
    def _():
        for q in range(4):
            @pl.when(n != q)
            def _():
                pltpu.make_async_copy(zin.at[q], zin.at[q], zinsem.at[q]).wait()

        @pl.loop(0, 2)
        def _(pair):
            z = jnp.concatenate(
                [
                    jnp.concatenate([zin[2 * pair + h, s] for s in range(PIECES)], axis=1)
                    for h in range(2)
                ],
                axis=0,
            )
            y = column_gate(z)
            for h in range(2):
                base = pl.multiple_of((2 * pair + h) * 2048, 2048)
                for ct in range(8):
                    out[pl.ds(base + ct, HALF, stride=8), :] = y[h * HALF:(h + 1) * HALF, ct * 128:(ct + 1) * 128]

    @pl.when(n1 == w5)
    def _():
        drain(512, ssem.at[0])
        drain(256, ssem.at[1])

    @pl.when(a_skipped)
    def _():
        drain(512 - PIECE, ssem.at[2])

    @pl.when((n1 == w5) & (w5 == 1))
    def _():
        drain(512 - STRAIGHT, ssem.at[2])

    @pl.when(n1 != w5)
    def _():
        drain(512, ssem.at[1])
        drain(256, ssem.at[2])

    @pl.when(a_straight)
    def _():
        drain(512 - PIECE, ssem.at[0])
        drain(PIECE, ssem.at[3])

    @pl.when((n1 != w5) & (w5 == 0))
    def _():
        drain(512 - STRAIGHT, ssem.at[0])
        drain(STRAIGHT, ssem.at[3])

    @pl.when(n0 == 0)
    def _():
        drain(576, zsem.at[0])

    @pl.when(n0 == 1)
    def _():
        drain(768, zsem.at[0])


def solution(mesh):
    half_wide = mesh.shape["wide"] // 2
    hbm = pl.BlockSpec(memory_space=pltpu.HBM)

    def local(state, col_blocks, row_blocks, col_pattern, row_pattern, qubit_order):
        result = pl.pallas_call(
            functools.partial(exchange, half_wide=half_wide),
            out_shape=jax.ShapeDtypeStruct((8 * N, LANES), F32),
            in_specs=[hbm] * 6,
            out_specs=pl.BlockSpec(memory_space=pltpu.VMEM),
            scratch_shapes=[
                pltpu.SMEM((1, NNZ), jnp.int32),
                pltpu.SMEM((1, NNZ), jnp.int32),
                pltpu.SMEM((1, 10), jnp.int32),
                pltpu.VMEM((NNZ * 128, LANES), F32),
                pltpu.VMEM((NNZ * 128, LANES), F32),
                pltpu.VMEM((PIECES, N, SLAB), F32),
                pltpu.VMEM((N, N), BF16),
                pltpu.VMEM((N, N), BF16),
                pltpu.VMEM((NNZ * 128, 2 * LANES), BF16),
                pltpu.VMEM((2 * NNZ * 128, 2 * LANES), BF16),
                pltpu.VMEM((N, N), BF16),
                pltpu.VMEM((N, N), BF16),
                pltpu.VMEM((2 * HALF, LANES), jnp.int32),
                pltpu.VMEM((256, NNZ * 128), BF16),
                pltpu.VMEM((PIECES, 2 * HALF, SLAB), F32),
                pltpu.VMEM((PIECES, HALF, SLAB), F32),
                pltpu.VMEM((4, PIECES, HALF, SLAB), F32),
                pltpu.VMEM((8 * N, LANES), F32),
                pltpu.VMEM((4 * N, LANES), F32),
                pltpu.SemaphoreType.DMA((FIRST + 5,)),
                pltpu.SemaphoreType.DMA((4,)),
                pltpu.SemaphoreType.DMA((FIRST + (TILES - 1) * PIECES + 1,)),
                pltpu.SemaphoreType.DMA((1,)),
                pltpu.SemaphoreType.DMA((4,)),
                pltpu.SemaphoreType.DMA((1,)),
            ],
            compiler_params=pltpu.CompilerParams(
                collective_id=0, has_side_effects=True, vmem_limit_bytes=48 << 20
            ),
        )(
            *(
                pltpu.with_memory_space_constraint(value, pltpu.HBM)
                for value in (
                    state,
                    col_blocks.reshape(NNZ * 128, LANES),
                    row_blocks.reshape(NNZ * 128, LANES),
                    col_pattern,
                    row_pattern,
                    qubit_order,
                )
            )
        )
        return result.reshape(N, 1, N)

    return jax.shard_map(
        local,
        mesh=mesh,
        in_specs=(P(("wide", "narrow"), None, None), P(), P(), P(), P(), P()),
        out_specs=P(("wide", "narrow"), None, None),
        check_vma=False,
    )
```

```python
import functools

import jax
import jax.numpy as jnp
from jax import lax
from jax.experimental import pallas as pl
from jax.experimental.pallas import tpu as pltpu
from jax.sharding import PartitionSpec as P

MESH = pl.DeviceIdType.MESH
F32, BF16 = jnp.float32, jnp.bfloat16
N = 1024
LANES = 128
NNZ = 16
TILES = 8
HALF = 64
PIECES = 4
PIECE = HALF // PIECES
SLAB = N // PIECES
FIRST = PIECES + 1
STRAIGHT = 6
LATE = 20


def split(value):
    hi = value.astype(BF16)
    lo = (value - hi.astype(F32)).astype(BF16)
    return hi, lo


def exchange(
    x_hbm, cb_hbm, rb_hbm, cpat_hbm, rpat_hbm, order_hbm, out,
    cpat, rpat, order, rbv, cbv, xraw, xhi, xlo, bcat, ccat, hhi, hlo, diff, acat,
    zs, zy, zin, ytile, ybuf, insem, ssem, ysem, zsem, zinsem, lsem, *, half_wide,
):
    w, n = lax.axis_index("wide"), lax.axis_index("narrow")
    w5, wl = w // half_wide, w % half_wide
    n1, n0 = n // 2, n % 2

    def place_of(a, b):
        return (a * half_wide + wl, b)

    barrier = pltpu.get_barrier_semaphore()
    pl.semaphore_signal(barrier, inc=1, device_id=place_of(1 - w5, n), device_id_type=MESH)
    for j in range(1, 4):
        pl.semaphore_signal(barrier, inc=1, device_id=place_of(w5, lax.rem(n + j, 4)), device_id_type=MESH)

    @pl.when(n1 != w5)
    def _():
        for j in range(2):
            pl.semaphore_signal(barrier, inc=1, device_id=place_of(1 - w5, 2 * w5 + j), device_id_type=MESH)

    def block(k):
        return pl.ds(pl.multiple_of(k * 128, 128), 128)

    def rows8(start, count):
        return pl.ds(pl.multiple_of(start * 8, 8), count * 8)

    def slab_copy(s):
        columns = pl.ds(pl.multiple_of(s * SLAB, SLAB), SLAB)
        return pltpu.make_async_copy(x_hbm.at[:, 0, columns], xraw.at[s], insem.at[s])

    def half_copy(h):
        return pltpu.make_async_copy(
            x_hbm.at[:, 0, pl.ds(h * 128, 128)], xraw.at[0, :, pl.ds(h * 128, 128)], insem.at[PIECES * h]
        )

    small = [
        pltpu.make_async_copy(source, target, insem.at[FIRST + q])
        for q, (source, target) in enumerate(((rpat_hbm, rpat), (cpat_hbm, cpat), (order_hbm, order)))
    ]
    rcopy = pltpu.make_async_copy(rb_hbm, rbv, insem.at[FIRST + 3])
    ccopy = pltpu.make_async_copy(cb_hbm, cbv, insem.at[FIRST + 4])
    for copy in small:
        copy.start()
    rcopy.start()
    for h in range(2):
        half_copy(h).start()
    for s in range(1, PIECES):
        slab_copy(s).start()
    ccopy.start()
    for copy in small:
        copy.wait()

    m = lax.broadcasted_iota(jnp.int32, (2 * HALF, LANES), 0)
    away = m // HALF
    label = (w5 + away - 2 * w5 * away) * (1 << order[0, 9])
    for q in range(6):
        label = label + ((m // (2**q)) % 2) * (1 << order[0, q])
    diff[...] = label - lax.broadcasted_iota(jnp.int32, (2 * HALF, LANES), 1)

    def pack(source, target):
        @pl.loop(0, NNZ)
        def _(k):
            hi, lo = split(source[block(k), :])
            target[block(k), 0:LANES] = hi
            target[block(k), LANES:2 * LANES] = lo

    def mixing(i):
        r8, j = i % 2, i // 2
        base = r8 * (1 << order[0, 8]) + (j % 2) * (1 << order[0, 6]) + (j // 2) * (1 << order[0, 7])
        for k in range(NNZ):
            onehot = (diff[...] == (rpat[0, k] >> 3) * 128 - base).astype(F32).astype(BF16)
            mixed = jnp.dot(onehot, bcat[k * 128:(k + 1) * 128, :], preferred_element_type=F32).astype(BF16)
            acat[0:128, k * 128:(k + 1) * 128] = mixed[:, :LANES]
            acat[128:256, k * 128:(k + 1) * 128] = mixed[:, LANES:]

    def row_gate(columns):
        total = None
        for k in range(0, NNZ, 2):
            left = acat[:, k * 128:(k + 2) * 128]
            first, second = pl.ds((rpat[0, k] & 7) * 128, 128), pl.ds((rpat[0, k + 1] & 7) * 128, 128)
            right = jnp.concatenate([xhi[first, columns], xhi[second, columns]], axis=0)
            both = jnp.dot(left, right, preferred_element_type=F32)
            right = jnp.concatenate([xlo[first, columns], xlo[second, columns]], axis=0)
            term = both[:128] + both[128:] + jnp.dot(left[:128], right, preferred_element_type=F32)
            total = term if total is None else total + term
        return total

    def column_gate(z):
        z_hi, z_lo = split(z)
        both = jnp.concatenate([z_hi, z_lo], axis=0)
        turned = (((1,), (1,)), ((), ()))
        both = lax.dot_general(both, hhi[...], turned, preferred_element_type=F32)
        return both[:128] + both[128:] + lax.dot_general(z_hi, hlo[...], turned, preferred_element_type=F32)

    def to_y(source, target, index):
        pltpu.make_async_remote_copy(
            src_ref=source, dst_ref=target, send_sem=ssem.at[0], recv_sem=ysem.at[index],
            device_id=place_of(1 - w5, n), device_id_type=MESH,
        ).start()

    def to_z(source, target, which, sem, column):
        pltpu.make_async_remote_copy(
            src_ref=source, dst_ref=target, send_sem=ssem.at[which], recv_sem=sem,
            device_id=place_of(w5, column), device_id_type=MESH,
        ).start()

    def make_part(s, lanes, copy):
        columns = pl.ds(pl.multiple_of(s * SLAB + lanes.start, 128), lanes.size)
        copy.wait()

        @pl.loop(0, N // 128)
        def _(b):
            hi, lo = split(xraw[s, block(b), lanes])
            xhi[block(b), columns] = hi
            xlo[block(b), columns] = lo

        zs[s, :, lanes] = row_gate(columns)

    def send_part(s, lanes, index):
        direct = (n1 == w5) & (n0 == 0)
        away_part, own_part = zs.at[s, pl.ds(HALF, HALF), lanes], zs.at[s, pl.ds(0, HALF), lanes]

        @pl.when(direct)
        def _():
            to_y(away_part, zin.at[n, s, :, lanes], index)
            pltpu.make_async_copy(own_part, zin.at[n, s, :, lanes], lsem.at[0]).start()

        @pl.when(jnp.logical_not(direct))
        def _():
            to_y(away_part, zy.at[s, :, lanes], index)
            to_z(own_part, zin.at[n, s, :, lanes], 1, zinsem.at[n], 2 * w5)

    def forward_part(s, lanes, index):
        source = zy.at[s, :, lanes]
        pltpu.make_async_copy(source, source, ysem.at[index]).wait()

        @pl.when(jnp.logical_not((n1 != w5) & (n0 == 0)))
        def _():
            to_z(source, zin.at[n, s, :, lanes], 2, zinsem.at[n], 2 * (1 - w5))

    def make_tile(i):
        mixing(i)
        y = column_gate(row_gate(slice(0, N)))
        base = pl.multiple_of(i * 1024, 1024)
        for ct in range(8):
            ytile[pl.ds(base + ct, 2 * HALF, stride=8), :] = y[:, ct * 128:(ct + 1) * 128]

    def spot(i):
        return (i % 2) * 256 + (i // 2) * HALF

    def y_index(i, p):
        return FIRST + (i - 1) * PIECES + p

    def away_piece(i, p, first, count, index):
        r8, j = i % 2, i // 2
        direct = (n1 == w5) & (n0 == r8)
        start = p * PIECE + first
        source = ytile.at[rows8(i * 128 + HALF + start, count)]

        @pl.when(direct)
        def _():
            to_y(source, out.at[rows8(n * 256 + j * HALF + start, count)], index)

        @pl.when(jnp.logical_not(direct))
        def _():
            to_y(source, ybuf.at[rows8(spot(i) + start, count)], index)

    last_a = (PIECES - 2, 2 * PIECE - LATE, LATE - STRAIGHT)
    last_b = (PIECES - 1, PIECE - STRAIGHT, STRAIGHT)
    a_straight = (n1 != w5) & (w5 == 1)
    a_skipped = (n1 == w5) & (w5 == 0)

    def straight(i, piece):
        r8, j = i % 2, i // 2
        p, first, count = piece
        start = p * PIECE + first
        pltpu.make_async_remote_copy(
            src_ref=ytile.at[rows8(i * 128 + HALF + start, count)],
            dst_ref=out.at[rows8(n * 256 + j * HALF + start, count)],
            send_sem=ssem.at[3], recv_sem=zsem.at[0],
            device_id=place_of(1 - w5, 2 * w5 + r8), device_id_type=MESH,
        ).start()

    def send_tile(i, last=False):
        r8, j = i % 2, i // 2
        direct = (n1 == w5) & (n0 == r8)
        mine = ytile.at[rows8(i * 128, HALF)]
        where = out.at[rows8(n * 256 + j * HALF, HALF)]
        for p in range(PIECES - 2 * last):
            away_piece(i, p, 0, PIECE, y_index(i, p))
        if last:
            away_piece(i, PIECES - 2, 0, 2 * PIECE - LATE, y_index(i, PIECES - 2))

            @pl.when(a_straight)
            def _():
                straight(i, last_a)

            @pl.when(jnp.logical_not(a_straight))
            def _():
                away_piece(i, *last_a, y_index(i, PIECES - 1))

            @pl.when(n1 != w5)
            def _():
                straight(i, last_b)

            @pl.when(n1 == w5)
            def _():
                away_piece(i, *last_b, y_index(i, PIECES))

        @pl.when(direct)
        def _():
            pltpu.make_async_copy(mine, where, lsem.at[0]).start()

        @pl.when(jnp.logical_not(direct))
        def _():
            to_z(mine, where, 1, zsem.at[0], 2 * w5 + r8)

    def forward(i, p, first=0, count=PIECE, index=None):
        r8, j = i % 2, i // 2
        start = p * PIECE + first
        source = ybuf.at[rows8(spot(i) + start, count)]
        pltpu.make_async_copy(source, source, ysem.at[y_index(i, p) if index is None else index]).wait()

        @pl.when(jnp.logical_not((n1 != w5) & (n0 == r8)))
        def _():
            target = out.at[rows8(n * 256 + j * HALF + start, count)]
            to_z(source, target, 2, zsem.at[0], 2 * (1 - w5) + r8)

    whole = pl.ds(0, SLAB)
    halves = (pl.ds(0, 128), pl.ds(128, 128))
    rcopy.wait()
    pack(rbv, bcat)
    mixing(0)
    make_part(0, halves[0], half_copy(0))

    @pl.when(n1 == w5)
    def _():
        pl.semaphore_wait(barrier, 4)

    @pl.when(n1 != w5)
    def _():
        pl.semaphore_wait(barrier, 6)

    def forward_when(side, s, lanes, index):
        @pl.when(w5 == side)
        def _():
            forward_part(s, lanes, index)

    send_part(0, halves[0], 0)
    forward_when(1, 0, halves[0], 0)
    make_part(0, halves[1], half_copy(1))
    send_part(0, halves[1], PIECES)
    forward_when(1, 0, halves[1], PIECES)
    make_part(1, whole, slab_copy(1))
    send_part(1, whole, 1)
    forward_when(0, 0, halves[0], 0)
    make_part(2, whole, slab_copy(2))
    send_part(2, whole, 2)
    forward_when(0, 0, halves[1], PIECES)
    make_part(3, whole, slab_copy(3))
    send_part(3, whole, 3)
    forward_part(1, whole, 1)
    ccopy.wait()
    pack(cbv, ccat)
    ccat[NNZ * 128:(NNZ + 1) * 128, :] = jnp.zeros((128, 2 * LANES), BF16)

    @pl.loop(0, 64)
    def _(q):
        found = NNZ
        for k in range(NNZ):
            found = found + (cpat[0, k] == q).astype(jnp.int32) * (k - NNZ)
        value = ccat[pl.ds((found & (2 * NNZ - 1)) * 128, 128), :]
        hhi[block(q // 8), block(q % 8)] = value[:, :LANES]
        hlo[block(q // 8), block(q % 8)] = value[:, LANES:]

    forward_part(2, whole, 2)

    @pl.loop(1, TILES - 1)
    def _(i):
        make_tile(i)
        send_tile(i)

        @pl.when(i == 1)
        def _():
            forward_part(3, whole, 3)

        @pl.when(i > 1)
        def _():
            for p in range(PIECES):
                forward(i - 1, p)

    make_tile(TILES - 1)
    send_tile(TILES - 1, last=True)
    for p in range(PIECES):
        forward(TILES - 2, p)
    for p in range(PIECES - 2):
        forward(TILES - 1, p)
    forward(TILES - 1, PIECES - 2, 0, 2 * PIECE - LATE)

    @pl.when(jnp.logical_not(a_skipped))
    def _():
        forward(TILES - 1, *last_a, y_index(TILES - 1, PIECES - 1))

    @pl.when(n1 != w5)
    def _():
        forward(TILES - 1, *last_b, y_index(TILES - 1, PIECES))

    def drain(rows, sem):
        ref = ytile.at[pl.ds(0, rows * 8)]
        pltpu.make_async_copy(ref, ref, sem).wait()

    @pl.when(n1 == w5)
    def _():
        drain(256, lsem.at[0])

    @pl.when(n0 == 0)
    def _():
        for q in range(4):
            @pl.when(n != q)
            def _():
                pltpu.make_async_copy(zin.at[q], zin.at[q], zinsem.at[q]).wait()

        @pl.loop(0, 2)
        def _(pair):
            z = jnp.concatenate(
                [
                    jnp.concatenate([zin[2 * pair + h, s] for s in range(PIECES)], axis=1)
                    for h in range(2)
                ],
                axis=0,
            )
            y = column_gate(z)
            for h in range(2):
                base = pl.multiple_of((2 * pair + h) * 2048, 2048)
                for ct in range(8):
                    out[pl.ds(base + ct, HALF, stride=8), :] = y[h * HALF:(h + 1) * HALF, ct * 128:(ct + 1) * 128]

    @pl.when(n1 == w5)
    def _():
        drain(512, ssem.at[0])
        drain(256, ssem.at[1])

    @pl.when(a_skipped)
    def _():
        drain(512 - LATE, ssem.at[2])

    @pl.when((n1 == w5) & (w5 == 1))
    def _():
        drain(512 - STRAIGHT, ssem.at[2])

    @pl.when(n1 != w5)
    def _():
        drain(512, ssem.at[1])
        drain(256, ssem.at[2])

    @pl.when(a_straight)
    def _():
        drain(512 - LATE, ssem.at[0])
        drain(LATE, ssem.at[3])

    @pl.when((n1 != w5) & (w5 == 0))
    def _():
        drain(512 - STRAIGHT, ssem.at[0])
        drain(STRAIGHT, ssem.at[3])

    @pl.when(n0 == 0)
    def _():
        drain(576, zsem.at[0])

    @pl.when(n0 == 1)
    def _():
        drain(768, zsem.at[0])


def solution(mesh):
    half_wide = mesh.shape["wide"] // 2
    hbm = pl.BlockSpec(memory_space=pltpu.HBM)

    def local(state, col_blocks, row_blocks, col_pattern, row_pattern, qubit_order):
        result = pl.pallas_call(
            functools.partial(exchange, half_wide=half_wide),
            out_shape=jax.ShapeDtypeStruct((8 * N, LANES), F32),
            in_specs=[hbm] * 6,
            out_specs=pl.BlockSpec(memory_space=pltpu.VMEM),
            scratch_shapes=[
                pltpu.SMEM((1, NNZ), jnp.int32),
                pltpu.SMEM((1, NNZ), jnp.int32),
                pltpu.SMEM((1, 10), jnp.int32),
                pltpu.VMEM((NNZ * 128, LANES), F32),
                pltpu.VMEM((NNZ * 128, LANES), F32),
                pltpu.VMEM((PIECES, N, SLAB), F32),
                pltpu.VMEM((N, N), BF16),
                pltpu.VMEM((N, N), BF16),
                pltpu.VMEM((NNZ * 128, 2 * LANES), BF16),
                pltpu.VMEM((2 * NNZ * 128, 2 * LANES), BF16),
                pltpu.VMEM((N, N), BF16),
                pltpu.VMEM((N, N), BF16),
                pltpu.VMEM((2 * HALF, LANES), jnp.int32),
                pltpu.VMEM((256, NNZ * 128), BF16),
                pltpu.VMEM((PIECES, 2 * HALF, SLAB), F32),
                pltpu.VMEM((PIECES, HALF, SLAB), F32),
                pltpu.VMEM((4, PIECES, HALF, SLAB), F32),
                pltpu.VMEM((8 * N, LANES), F32),
                pltpu.VMEM((4 * N, LANES), F32),
                pltpu.SemaphoreType.DMA((FIRST + 5,)),
                pltpu.SemaphoreType.DMA((4,)),
                pltpu.SemaphoreType.DMA((FIRST + (TILES - 1) * PIECES + 1,)),
                pltpu.SemaphoreType.DMA((1,)),
                pltpu.SemaphoreType.DMA((4,)),
                pltpu.SemaphoreType.DMA((1,)),
            ],
            compiler_params=pltpu.CompilerParams(
                collective_id=0, has_side_effects=True, vmem_limit_bytes=48 << 20
            ),
        )(
            *(
                pltpu.with_memory_space_constraint(value, pltpu.HBM)
                for value in (
                    state,
                    col_blocks.reshape(NNZ * 128, LANES),
                    row_blocks.reshape(NNZ * 128, LANES),
                    col_pattern,
                    row_pattern,
                    qubit_order,
                )
            )
        )
        return result.reshape(N, 1, N)

    return jax.shard_map(
        local,
        mesh=mesh,
        in_specs=(P(("wide", "narrow"), None, None), P(), P(), P(), P(), P()),
        out_specs=P(("wide", "narrow"), None, None),
        check_vma=False,
    )
```

```python
import functools

import jax
import jax.numpy as jnp
from jax import lax
from jax.experimental import pallas as pl
from jax.experimental.pallas import tpu as pltpu
from jax.sharding import PartitionSpec as P

MESH = pl.DeviceIdType.MESH
F32, BF16 = jnp.float32, jnp.bfloat16
N = 1024
LANES = 128
NNZ = 16
TILES = 8
HALF = 64
PIECES = 4
PIECE = HALF // PIECES
SLAB = N // PIECES
FIRST = PIECES + 1
STRAIGHT = 6


def split(value):
    hi = value.astype(BF16)
    lo = (value - hi.astype(F32)).astype(BF16)
    return hi, lo


def exchange(
    x_hbm, cb_hbm, rb_hbm, cpat_hbm, rpat_hbm, order_hbm, out,
    cpat, rpat, order, rbv, cbv, xraw, xhi, xlo, bcat, ccat, hhi, hlo, diff, acat,
    zs, zy, zin, ytile, ybuf, insem, ssem, ysem, zsem, zinsem, lsem, *, half_wide,
):
    w, n = lax.axis_index("wide"), lax.axis_index("narrow")
    w5, wl = w // half_wide, w % half_wide
    n1, n0 = n // 2, n % 2

    def place_of(a, b):
        return (a * half_wide + wl, b)

    barrier = pltpu.get_barrier_semaphore()
    pl.semaphore_signal(barrier, inc=1, device_id=place_of(1 - w5, n), device_id_type=MESH)
    for j in range(1, 4):
        pl.semaphore_signal(barrier, inc=1, device_id=place_of(w5, lax.rem(n + j, 4)), device_id_type=MESH)

    @pl.when(n1 != w5)
    def _():
        for j in range(2):
            pl.semaphore_signal(barrier, inc=1, device_id=place_of(1 - w5, 2 * w5 + j), device_id_type=MESH)

    def block(k):
        return pl.ds(pl.multiple_of(k * 128, 128), 128)

    def rows8(start, count):
        return pl.ds(pl.multiple_of(start * 8, 8), count * 8)

    def slab_copy(s):
        columns = pl.ds(pl.multiple_of(s * SLAB, SLAB), SLAB)
        return pltpu.make_async_copy(x_hbm.at[:, 0, columns], xraw.at[s], insem.at[s])

    def half_copy(h):
        return pltpu.make_async_copy(
            x_hbm.at[:, 0, pl.ds(h * 128, 128)], xraw.at[0, :, pl.ds(h * 128, 128)], insem.at[PIECES * h]
        )

    small = [
        pltpu.make_async_copy(source, target, insem.at[FIRST + q])
        for q, (source, target) in enumerate(((rpat_hbm, rpat), (cpat_hbm, cpat), (order_hbm, order)))
    ]
    rcopy = pltpu.make_async_copy(rb_hbm, rbv, insem.at[FIRST + 3])
    ccopy = pltpu.make_async_copy(cb_hbm, cbv, insem.at[FIRST + 4])
    for copy in small:
        copy.start()
    rcopy.start()
    for h in range(2):
        half_copy(h).start()
    for s in range(1, PIECES):
        slab_copy(s).start()
    ccopy.start()
    for copy in small:
        copy.wait()

    m = lax.broadcasted_iota(jnp.int32, (2 * HALF, LANES), 0)
    away = m // HALF
    label = (w5 + away - 2 * w5 * away) * (1 << order[0, 9])
    for q in range(6):
        label = label + ((m // (2**q)) % 2) * (1 << order[0, q])
    diff[...] = label - lax.broadcasted_iota(jnp.int32, (2 * HALF, LANES), 1)

    def pack(source, target):
        @pl.loop(0, NNZ)
        def _(k):
            hi, lo = split(source[block(k), :])
            target[block(k), 0:LANES] = hi
            target[block(k), LANES:2 * LANES] = lo

    def mixing(i):
        r8, j = i % 2, i // 2
        base = r8 * (1 << order[0, 8]) + (j % 2) * (1 << order[0, 6]) + (j // 2) * (1 << order[0, 7])
        for k in range(NNZ):
            onehot = (diff[...] == (rpat[0, k] >> 3) * 128 - base).astype(F32).astype(BF16)
            mixed = jnp.dot(onehot, bcat[k * 128:(k + 1) * 128, :], preferred_element_type=F32).astype(BF16)
            acat[0:128, k * 128:(k + 1) * 128] = mixed[:, :LANES]
            acat[128:256, k * 128:(k + 1) * 128] = mixed[:, LANES:]

    def row_gate(columns):
        total = None
        for k in range(0, NNZ, 2):
            left = acat[:, k * 128:(k + 2) * 128]
            first, second = pl.ds((rpat[0, k] & 7) * 128, 128), pl.ds((rpat[0, k + 1] & 7) * 128, 128)
            right = jnp.concatenate([xhi[first, columns], xhi[second, columns]], axis=0)
            both = jnp.dot(left, right, preferred_element_type=F32)
            right = jnp.concatenate([xlo[first, columns], xlo[second, columns]], axis=0)
            term = both[:128] + both[128:] + jnp.dot(left[:128], right, preferred_element_type=F32)
            total = term if total is None else total + term
        return total

    def column_gate(z):
        z_hi, z_lo = split(z)
        both = jnp.concatenate([z_hi, z_lo], axis=0)
        turned = (((1,), (1,)), ((), ()))
        both = lax.dot_general(both, hhi[...], turned, preferred_element_type=F32)
        return both[:128] + both[128:] + lax.dot_general(z_hi, hlo[...], turned, preferred_element_type=F32)

    def to_y(source, target, index):
        pltpu.make_async_remote_copy(
            src_ref=source, dst_ref=target, send_sem=ssem.at[0], recv_sem=ysem.at[index],
            device_id=place_of(1 - w5, n), device_id_type=MESH,
        ).start()

    def to_z(source, target, which, sem, column):
        pltpu.make_async_remote_copy(
            src_ref=source, dst_ref=target, send_sem=ssem.at[which], recv_sem=sem,
            device_id=place_of(w5, column), device_id_type=MESH,
        ).start()

    def make_part(s, lanes, copy):
        columns = pl.ds(pl.multiple_of(s * SLAB + lanes.start, 128), lanes.size)
        copy.wait()

        @pl.loop(0, N // 128)
        def _(b):
            hi, lo = split(xraw[s, block(b), lanes])
            xhi[block(b), columns] = hi
            xlo[block(b), columns] = lo

        zs[s, :, lanes] = row_gate(columns)

    def send_part(s, lanes, index):
        direct = (n1 == w5) & (n0 == 0)
        away_part, own_part = zs.at[s, pl.ds(HALF, HALF), lanes], zs.at[s, pl.ds(0, HALF), lanes]

        @pl.when(direct)
        def _():
            to_y(away_part, zin.at[n, s, :, lanes], index)
            pltpu.make_async_copy(own_part, zin.at[n, s, :, lanes], lsem.at[0]).start()

        @pl.when(jnp.logical_not(direct))
        def _():
            to_y(away_part, zy.at[s, :, lanes], index)
            to_z(own_part, zin.at[n, s, :, lanes], 1, zinsem.at[n], 2 * w5)

    def forward_part(s, lanes, index):
        source = zy.at[s, :, lanes]
        pltpu.make_async_copy(source, source, ysem.at[index]).wait()

        @pl.when(jnp.logical_not((n1 != w5) & (n0 == 0)))
        def _():
            to_z(source, zin.at[n, s, :, lanes], 2, zinsem.at[n], 2 * (1 - w5))

    def make_tile(i):
        mixing(i)
        y = column_gate(row_gate(slice(0, N)))
        base = pl.multiple_of(i * 1024, 1024)
        for ct in range(8):
            ytile[pl.ds(base + ct, 2 * HALF, stride=8), :] = y[:, ct * 128:(ct + 1) * 128]

    def spot(i):
        return (i % 2) * 256 + (i // 2) * HALF

    def y_index(i, p):
        return FIRST + (i - 1) * PIECES + p

    def away_piece(i, p, first, count, index):
        r8, j = i % 2, i // 2
        direct = (n1 == w5) & (n0 == r8)
        start = p * PIECE + first
        source = ytile.at[rows8(i * 128 + HALF + start, count)]

        @pl.when(direct)
        def _():
            to_y(source, out.at[rows8(n * 256 + j * HALF + start, count)], index)

        @pl.when(jnp.logical_not(direct))
        def _():
            to_y(source, ybuf.at[rows8(spot(i) + start, count)], index)

    last_a = (PIECES - 1, 0, PIECE - STRAIGHT)
    last_b = (PIECES - 1, PIECE - STRAIGHT, STRAIGHT)
    a_straight = (n1 != w5) & (w5 == 1)
    a_skipped = (n1 == w5) & (w5 == 0)

    def straight(i, piece):
        r8, j = i % 2, i // 2
        p, first, count = piece
        start = p * PIECE + first
        pltpu.make_async_remote_copy(
            src_ref=ytile.at[rows8(i * 128 + HALF + start, count)],
            dst_ref=out.at[rows8(n * 256 + j * HALF + start, count)],
            send_sem=ssem.at[3], recv_sem=zsem.at[0],
            device_id=place_of(1 - w5, 2 * w5 + r8), device_id_type=MESH,
        ).start()

    def send_tile(i, last=False):
        r8, j = i % 2, i // 2
        direct = (n1 == w5) & (n0 == r8)
        mine = ytile.at[rows8(i * 128, HALF)]
        where = out.at[rows8(n * 256 + j * HALF, HALF)]
        for p in range(PIECES - last):
            away_piece(i, p, 0, PIECE, y_index(i, p))
        if last:
            @pl.when(a_straight)
            def _():
                straight(i, last_a)

            @pl.when(jnp.logical_not(a_straight))
            def _():
                away_piece(i, *last_a, y_index(i, PIECES - 1))

            @pl.when(n1 != w5)
            def _():
                straight(i, last_b)

            @pl.when(n1 == w5)
            def _():
                away_piece(i, *last_b, y_index(i, PIECES))

        @pl.when(direct)
        def _():
            pltpu.make_async_copy(mine, where, lsem.at[0]).start()

        @pl.when(jnp.logical_not(direct))
        def _():
            to_z(mine, where, 1, zsem.at[0], 2 * w5 + r8)

    def forward(i, p, first=0, count=PIECE, index=None):
        r8, j = i % 2, i // 2
        start = p * PIECE + first
        source = ybuf.at[rows8(spot(i) + start, count)]
        pltpu.make_async_copy(source, source, ysem.at[y_index(i, p) if index is None else index]).wait()

        @pl.when(jnp.logical_not((n1 != w5) & (n0 == r8)))
        def _():
            target = out.at[rows8(n * 256 + j * HALF + start, count)]
            to_z(source, target, 2, zsem.at[0], 2 * (1 - w5) + r8)

    whole = pl.ds(0, SLAB)
    halves = (pl.ds(0, 128), pl.ds(128, 128))
    rcopy.wait()
    pack(rbv, bcat)
    mixing(0)
    make_part(0, halves[0], half_copy(0))

    @pl.when(n1 == w5)
    def _():
        pl.semaphore_wait(barrier, 4)

    @pl.when(n1 != w5)
    def _():
        pl.semaphore_wait(barrier, 6)

    send_part(0, halves[0], 0)
    make_part(0, halves[1], half_copy(1))
    send_part(0, halves[1], PIECES)
    make_part(1, whole, slab_copy(1))
    send_part(1, whole, 1)
    make_part(2, whole, slab_copy(2))
    send_part(2, whole, 2)
    make_part(3, whole, slab_copy(3))
    send_part(3, whole, 3)
    forward_part(0, halves[0], 0)
    forward_part(0, halves[1], PIECES)
    forward_part(1, whole, 1)
    ccopy.wait()
    pack(cbv, ccat)
    ccat[NNZ * 128:(NNZ + 1) * 128, :] = jnp.zeros((128, 2 * LANES), BF16)

    @pl.loop(0, 64)
    def _(q):
        found = NNZ
        for k in range(NNZ):
            found = found + (cpat[0, k] == q).astype(jnp.int32) * (k - NNZ)
        value = ccat[pl.ds((found & (2 * NNZ - 1)) * 128, 128), :]
        hhi[block(q // 8), block(q % 8)] = value[:, :LANES]
        hlo[block(q // 8), block(q % 8)] = value[:, LANES:]

    forward_part(2, whole, 2)

    @pl.loop(1, TILES - 1)
    def _(i):
        make_tile(i)
        send_tile(i)

        @pl.when(i == 1)
        def _():
            forward_part(3, whole, 3)

        @pl.when(i > 1)
        def _():
            for p in range(PIECES):
                forward(i - 1, p)

    make_tile(TILES - 1)
    send_tile(TILES - 1, last=True)
    for p in range(PIECES):
        forward(TILES - 2, p)
    for p in range(PIECES - 1):
        forward(TILES - 1, p)

    @pl.when(jnp.logical_not(a_skipped))
    def _():
        forward(TILES - 1, *last_a)

    @pl.when(n1 != w5)
    def _():
        forward(TILES - 1, *last_b, y_index(TILES - 1, PIECES))

    def drain(rows, sem):
        ref = ytile.at[pl.ds(0, rows * 8)]
        pltpu.make_async_copy(ref, ref, sem).wait()

    @pl.when(n1 == w5)
    def _():
        drain(256, lsem.at[0])

    @pl.when(n0 == 0)
    def _():
        for q in range(4):
            @pl.when(n != q)
            def _():
                pltpu.make_async_copy(zin.at[q], zin.at[q], zinsem.at[q]).wait()

        @pl.loop(0, 2)
        def _(pair):
            z = jnp.concatenate(
                [
                    jnp.concatenate([zin[2 * pair + h, s] for s in range(PIECES)], axis=1)
                    for h in range(2)
                ],
                axis=0,
            )
            y = column_gate(z)
            for h in range(2):
                base = pl.multiple_of((2 * pair + h) * 2048, 2048)
                for ct in range(8):
                    out[pl.ds(base + ct, HALF, stride=8), :] = y[h * HALF:(h + 1) * HALF, ct * 128:(ct + 1) * 128]

    @pl.when(n1 == w5)
    def _():
        drain(512, ssem.at[0])
        drain(256, ssem.at[1])

    @pl.when(a_skipped)
    def _():
        drain(512 - PIECE, ssem.at[2])

    @pl.when((n1 == w5) & (w5 == 1))
    def _():
        drain(512 - STRAIGHT, ssem.at[2])

    @pl.when(n1 != w5)
    def _():
        drain(512, ssem.at[1])
        drain(256, ssem.at[2])

    @pl.when(a_straight)
    def _():
        drain(512 - PIECE, ssem.at[0])
        drain(PIECE, ssem.at[3])

    @pl.when((n1 != w5) & (w5 == 0))
    def _():
        drain(512 - STRAIGHT, ssem.at[0])
        drain(STRAIGHT, ssem.at[3])

    @pl.when(n0 == 0)
    def _():
        drain(576, zsem.at[0])

    @pl.when(n0 == 1)
    def _():
        drain(768, zsem.at[0])


def solution(mesh):
    half_wide = mesh.shape["wide"] // 2
    hbm = pl.BlockSpec(memory_space=pltpu.HBM)

    def local(state, col_blocks, row_blocks, col_pattern, row_pattern, qubit_order):
        result = pl.pallas_call(
            functools.partial(exchange, half_wide=half_wide),
            out_shape=jax.ShapeDtypeStruct((8 * N, LANES), F32),
            in_specs=[hbm] * 6,
            out_specs=pl.BlockSpec(memory_space=pltpu.VMEM),
            scratch_shapes=[
                pltpu.SMEM((1, NNZ), jnp.int32),
                pltpu.SMEM((1, NNZ), jnp.int32),
                pltpu.SMEM((1, 10), jnp.int32),
                pltpu.VMEM((NNZ * 128, LANES), F32),
                pltpu.VMEM((NNZ * 128, LANES), F32),
                pltpu.VMEM((PIECES, N, SLAB), F32),
                pltpu.VMEM((N, N), BF16),
                pltpu.VMEM((N, N), BF16),
                pltpu.VMEM((NNZ * 128, 2 * LANES), BF16),
                pltpu.VMEM((2 * NNZ * 128, 2 * LANES), BF16),
                pltpu.VMEM((N, N), BF16),
                pltpu.VMEM((N, N), BF16),
                pltpu.VMEM((2 * HALF, LANES), jnp.int32),
                pltpu.VMEM((256, NNZ * 128), BF16),
                pltpu.VMEM((PIECES, 2 * HALF, SLAB), F32),
                pltpu.VMEM((PIECES, HALF, SLAB), F32),
                pltpu.VMEM((4, PIECES, HALF, SLAB), F32),
                pltpu.VMEM((8 * N, LANES), F32),
                pltpu.VMEM((4 * N, LANES), F32),
                pltpu.SemaphoreType.DMA((FIRST + 5,)),
                pltpu.SemaphoreType.DMA((4,)),
                pltpu.SemaphoreType.DMA((FIRST + (TILES - 1) * PIECES + 1,)),
                pltpu.SemaphoreType.DMA((1,)),
                pltpu.SemaphoreType.DMA((4,)),
                pltpu.SemaphoreType.DMA((1,)),
            ],
            compiler_params=pltpu.CompilerParams(
                collective_id=0, has_side_effects=True, vmem_limit_bytes=48 << 20
            ),
        )(
            *(
                pltpu.with_memory_space_constraint(value, pltpu.HBM)
                for value in (
                    state,
                    col_blocks.reshape(NNZ * 128, LANES),
                    row_blocks.reshape(NNZ * 128, LANES),
                    col_pattern,
                    row_pattern,
                    qubit_order,
                )
            )
        )
        return result.reshape(N, 1, N)

    return jax.shard_map(
        local,
        mesh=mesh,
        in_specs=(P(("wide", "narrow"), None, None), P(), P(), P(), P(), P()),
        out_specs=P(("wide", "narrow"), None, None),
        check_vma=False,
    )
```
